128 devices in a mesh: dp: 4 (over z_lo, core), expert: 32 (over x, y, z_hi).
Axes of the slice: x: 4, y: 4, z: 4 (z_hi: 2, z_lo: 2; z = z_hi * 2 + z_lo), core: 2. Of those that a mesh axis runs over, the one named last changes fastest.
Arguments:
- tokens: bfloat16 [256, 256, 1280], P(('dp', 'expert')), may hold values from -8 to 8
- router: bfloat16 [128, 1280], P(('dp', 'expert')), may hold values from -28.36068 to 28.36068
- w_in: bfloat16 [128, 1280, 2560], P('expert', None, 'dp'), may hold values from -0.15625 to 0.15625
- w_out: bfloat16 [128, 2560, 1280], P('expert', 'dp'), may hold values from -0.125 to 0.125
- d_out: bfloat16 [256, 256, 1280], P(('dp', 'expert')), may hold values from -6 to 6
Outputs:
- d_tokens: bfloat16 [256, 256, 1280], P(('dp', 'expert'))
- d_router: float32 [128, 1280], P(('dp', 'expert'))
- d_w_out: bfloat16 [128, 2560, 1280], P('expert', 'dp')
The draws below stay inside these ranges and needn't reach their ends.
All inputs are finite; a program needn't handle non-finite values.
Results may differ from the reference program's by a relative error of at most 0.019.
Values may be sent and summed in bfloat16 or wider, within the bound.
No kernel may reach another device: no remote copies, remote signals or barrier semaphores. Data moves between devices by JAX's collectives and lax.ppermute only.
A program may use at most 128 MiB of HBM per device.

```python
import math
import jax
import jax.numpy as jnp
from jax import lax

D = 1280
M = 256
FF = 2560
EXPERTS = 128
IMAGES = 256
N_DP = 4


def draw_tokens(key, part):
    key = jax.random.fold_in(key, 11)
    values = jax.random.truncated_normal(key, -6.0, 6.0, (IMAGES, M, D), jnp.float32)
    return values.astype(jnp.bfloat16)


def draw_router(key, part):
    key = jax.random.fold_in(key, 13)
    values = 1.5 * jax.random.truncated_normal(key, -4.0, 4.0, (EXPERTS, D), jnp.float32)
    return values.astype(jnp.bfloat16)


def shard_levels(own_key, extent, shards, least, largest):
    loudness = 1.0
    for dim, shards_of in shards:
        draws = jax.random.uniform(jax.random.fold_in(jax.random.fold_in(own_key, 6), dim), (shards_of,), jnp.float32, least / len(shards), largest / len(shards))
        loudness = loudness * jnp.repeat(jnp.exp(draws), extent[dim] // shards_of).reshape((-1,) + (1,) * (len(extent) - 1 - dim))
    return loudness


def centred(stream_key, extent, deviation, limit, pieces=(), kind=jnp.bfloat16):
    drawn = jax.random.normal(stream_key, extent, jnp.float32) * deviation
    if len(pieces) > 0:
        drawn = shard_levels(stream_key, extent, pieces, -0.22, 0.18) * drawn
    return jnp.clip(drawn, min=-limit, max=limit).astype(kind)


def setup_inputs(seed: int = 0) -> dict:
    streams_of = jax.random.split(jax.random.key(seed), 6)
    return {
        "tokens": draw_tokens(jax.random.fold_in(streams_of[5], 71), 0),
        "router": draw_router(jax.random.fold_in(streams_of[5], 71), 0),
        "w_in": centred(streams_of[2], (EXPERTS, D, FF), D ** -0.5, 0.15625, ((0, 32), (2, 4))),
        "w_out": centred(streams_of[3], (EXPERTS, FF, D), FF ** -0.5, 0.125, ((0, 32), (1, 4))),
        "d_out": centred(streams_of[4], (IMAGES, M, D), 1.0, 6.0, ((0, 128),)),
    }


def gelu_exact(values):
    return jax.nn.gelu(values, approximate=False)

def rounded_total(terms):
    halves = lax.optimization_barrier(terms.astype(jnp.bfloat16))
    return lax.optimization_barrier(jnp.sum(halves.astype(jnp.float32), axis=0)).astype(jnp.bfloat16)

def softmax_both(tokens_one, router):
    logits = jnp.dot(tokens_one, router.T, preferred_element_type=jnp.float32) * (1.0 / math.sqrt(D))
    return (jax.nn.softmax(logits, axis=0), jax.nn.softmax(logits, axis=1))

def reference(tokens, router, w_in, w_out, d_out):
    block_ff = FF // N_DP

    def forward_one(item):
        tokens_one, grad_one = item
        dispatch, combine = softmax_both(tokens_one, router)
        slot_one = jnp.dot(dispatch.astype(jnp.bfloat16).T, tokens_one, preferred_element_type=jnp.float32).astype(jnp.bfloat16)
        grad_slot = jnp.dot(combine.astype(jnp.bfloat16).T, grad_one, preferred_element_type=jnp.float32).astype(jnp.bfloat16)
        return (slot_one, grad_slot)
    slots, slot_grads = lax.map(forward_one, (tokens, d_out))

    def expert_one(item):
        slot_in, grad_in, weight_in, weight_out = item
        before = jnp.dot(slot_in, weight_in, preferred_element_type=jnp.float32)
        active, backward = jax.vjp(gelu_exact, before)
        active_rounded = active.astype(jnp.bfloat16)
        out_terms = jnp.einsum('rkf,kfd->krd', active_rounded.astype(jnp.float32).reshape(IMAGES, N_DP, block_ff), weight_out.astype(jnp.float32).reshape(N_DP, block_ff, D))
        expert_out = rounded_total(out_terms)
        grad_active = jnp.dot(grad_in, weight_out.T, preferred_element_type=jnp.float32)
        grad_before = backward(grad_active)[0].astype(jnp.bfloat16)
        weight_grad = jnp.dot(active_rounded.T, grad_in, preferred_element_type=jnp.float32).astype(jnp.bfloat16)
        back_terms = jnp.einsum('rkf,dkf->krd', grad_before.astype(jnp.float32).reshape(IMAGES, N_DP, block_ff), weight_in.astype(jnp.float32).reshape(D, N_DP, block_ff))
        return (expert_out, rounded_total(back_terms), weight_grad)
    outputs, slot_back, d_w_out = lax.map(expert_one, (jnp.transpose(slots, (1, 0, 2)), jnp.transpose(slot_grads, (1, 0, 2)), w_in, w_out))
    outputs = jnp.transpose(outputs, (1, 0, 2))
    slot_back = jnp.transpose(slot_back, (1, 0, 2))

    def backward_one(total, item):
        tokens_one, grad_one, expert_out, slot_grad = item
        dispatch, combine = softmax_both(tokens_one, router)
        dispatch_rounded = dispatch.astype(jnp.bfloat16)
        grad_combine = jnp.dot(grad_one, expert_out.T, preferred_element_type=jnp.float32)
        combine_part = combine * (grad_combine - lax.optimization_barrier(jnp.sum(combine * grad_combine, axis=1, keepdims=True)))
        grad_dispatch = jnp.dot(tokens_one, slot_grad.T, preferred_element_type=jnp.float32)
        dispatch_part = dispatch * (grad_dispatch - lax.optimization_barrier(jnp.sum(dispatch * grad_dispatch, axis=0, keepdims=True)))
        logit_grad = ((combine_part + dispatch_part) * (1.0 / math.sqrt(D))).astype(jnp.bfloat16)
        token_grad = (jnp.dot(dispatch_rounded, slot_grad, preferred_element_type=jnp.float32) + jnp.dot(logit_grad, router, preferred_element_type=jnp.float32)).astype(jnp.bfloat16)
        total = total + jnp.dot(logit_grad.T, tokens_one, preferred_element_type=jnp.float32)
        return (total, token_grad)
    d_router, d_tokens = lax.scan(backward_one, jnp.zeros((EXPERTS, D), jnp.float32), (tokens, d_out, outputs, slot_back))
    return (d_tokens, d_router, d_w_out)
```

```python
import math

import jax
import jax.numpy as jnp
from jax import lax
from jax.sharding import PartitionSpec as P


def gather_router(router):
    rows = lax.axis_size(("dp", "expert")) * router.shape[0]
    spread = jnp.broadcast_to(router, (rows, router.shape[1]))
    return lax.all_to_all(spread, ("dp", "expert"), split_axis=0, concat_axis=0, tiled=True)


def reduce_router(router_term):
    received = lax.all_to_all(
        router_term.astype(jnp.bfloat16), ("dp", "expert"), split_axis=0, concat_axis=0, tiled=True
    )
    return jnp.sum(received.astype(jnp.float32), axis=0, keepdims=True)


def send_in(payload):
    return (
        lax.all_to_all(payload[0], "expert", split_axis=1, concat_axis=0, tiled=True),
        lax.all_to_all(payload[1], "expert", split_axis=1, concat_axis=0, tiled=True),
    )


def spread_in(payload):
    return (
        lax.all_gather(payload[0], "dp", axis=0, tiled=True),
        lax.all_gather(payload[1], "dp", axis=0, tiled=True),
    )


def share_out(payload):
    groups = lax.axis_size("dp")
    first_blocks = payload[0].reshape(
        (groups, payload[0].shape[0] // groups) + payload[0].shape[1:]
    )
    second_blocks = payload[1].reshape(
        (groups, payload[1].shape[0] // groups) + payload[1].shape[1:]
    )
    received = (
        lax.all_to_all(first_blocks, "dp", split_axis=0, concat_axis=0, tiled=True),
        lax.all_to_all(second_blocks, "dp", split_axis=0, concat_axis=0, tiled=True),
    )
    return (
        jnp.sum(received[0].astype(jnp.float32), axis=0).astype(jnp.bfloat16),
        jnp.sum(received[1].astype(jnp.float32), axis=0).astype(jnp.bfloat16),
    )


def send_out(payload):
    return (
        lax.all_to_all(payload[0], "expert", split_axis=0, concat_axis=1, tiled=True),
        lax.all_to_all(payload[1], "expert", split_axis=0, concat_axis=1, tiled=True),
    )


def body(tokens, router, w_in, w_out, d_out):
    score_scale = 1.0 / math.sqrt(tokens.shape[2])
    router_full = gather_router(router)
    logits = (
        jnp.einsum("imd,nd->imn", tokens, router_full, preferred_element_type=jnp.float32)
        * score_scale
    )
    combine = jax.nn.softmax(logits, axis=2)
    dispatch = jax.nn.softmax(logits, axis=1)
    dispatch_rounded = dispatch.astype(jnp.bfloat16)
    combine_rounded = combine.astype(jnp.bfloat16)
    slot_part = jnp.einsum(
        "imn,imd->ind", dispatch_rounded, tokens, preferred_element_type=jnp.float32
    ).astype(jnp.bfloat16)
    grad_part = jnp.einsum(
        "imn,imd->ind", combine_rounded, d_out, preferred_element_type=jnp.float32
    ).astype(jnp.bfloat16)
    slots, slot_grads = spread_in(send_in((slot_part, grad_part)))
    before = jnp.einsum("red,edf->ref", slots, w_in, preferred_element_type=jnp.float32)
    active, backward = jax.vjp(lambda values: jax.nn.gelu(values, approximate=False), before)
    active_rounded = active.astype(jnp.bfloat16)
    out_part = jnp.einsum(
        "ref,efd->red", active_rounded, w_out, preferred_element_type=jnp.float32
    ).astype(jnp.bfloat16)
    grad_active = jnp.einsum("red,efd->ref", slot_grads, w_out, preferred_element_type=jnp.float32)
    grad_before = backward(grad_active)[0].astype(jnp.bfloat16)
    d_w_out = jnp.einsum(
        "ref,red->efd", active_rounded, slot_grads, preferred_element_type=jnp.float32
    ).astype(jnp.bfloat16)
    back_part = jnp.einsum(
        "ref,edf->red", grad_before, w_in, preferred_element_type=jnp.float32
    ).astype(jnp.bfloat16)
    expert_out, slot_back = send_out(share_out((out_part, back_part)))
    grad_combine = jnp.einsum("imd,ind->imn", d_out, expert_out, preferred_element_type=jnp.float32)
    combine_part = combine * (grad_combine - jnp.sum(combine * grad_combine, axis=2, keepdims=True))
    grad_dispatch = jnp.einsum(
        "imd,ind->imn", tokens, slot_back, preferred_element_type=jnp.float32
    )
    dispatch_part = dispatch * (
        grad_dispatch - jnp.sum(dispatch * grad_dispatch, axis=1, keepdims=True)
    )
    logit_grad = ((combine_part + dispatch_part) * score_scale).astype(jnp.bfloat16)
    d_tokens = (
        jnp.einsum("imn,ind->imd", dispatch_rounded, slot_back, preferred_element_type=jnp.float32)
        + jnp.einsum("imn,nd->imd", logit_grad, router_full, preferred_element_type=jnp.float32)
    ).astype(jnp.bfloat16)
    router_term = jnp.einsum("imn,imd->nd", logit_grad, tokens, preferred_element_type=jnp.float32)
    d_router = reduce_router(router_term)
    return (d_tokens, d_router, d_w_out)


def solution(mesh):
    placed = (
        P(("dp", "expert"), None, None),
        P(("dp", "expert"), None),
        P("expert", None, "dp"),
        P("expert", "dp", None),
        P(("dp", "expert"), None, None),
    )
    return jax.shard_map(
        body,
        mesh=mesh,
        in_specs=placed,
        out_specs=(
            P(("dp", "expert"), None, None),
            P(("dp", "expert"), None),
            P("expert", "dp", None),
        ),
        check_vma=False,
    )
```

```python
import math

import jax
import jax.numpy as jnp
from jax import lax
from jax.sharding import PartitionSpec as P

ALL = ("dp", "expert")
CHIP = [(index, index ^ 2) for index in range(4)]
CORE = [(index, index ^ 1) for index in range(4)]


def gather_router(router):
    rows = lax.axis_size(ALL) * router.shape[0]
    spread = jnp.broadcast_to(router, (rows, router.shape[1]))
    return lax.all_to_all(spread, ALL, split_axis=0, concat_axis=0, tiled=True)


def reduce_router(router_term):
    received = lax.all_to_all(
        router_term.astype(jnp.bfloat16), ALL, split_axis=0, concat_axis=0, tiled=True
    )
    return jnp.sum(received.astype(jnp.float32), axis=0, keepdims=True)


def send_in(part):
    groups = lax.axis_size("expert")
    images, slots, width = part.shape
    blocks = part.transpose(1, 0, 2).reshape(groups, slots // groups * images, width)
    blocks = lax.all_to_all(blocks, "expert", split_axis=0, concat_axis=0, tiled=True)
    blocks = blocks.reshape(groups, slots // groups, images, width)
    return blocks.transpose(1, 0, 2, 3).reshape(slots // groups, groups * images, width)


def send_out(rows, images):
    groups = lax.axis_size("expert")
    experts, count, width = rows.shape
    blocks = rows.reshape(experts, groups, images, width).transpose(1, 0, 2, 3)
    blocks = blocks.reshape(groups, experts * images, width)
    blocks = lax.all_to_all(blocks, "expert", split_axis=0, concat_axis=0, tiled=True)
    blocks = blocks.reshape(groups * experts, images, width)
    return blocks.transpose(1, 0, 2)


def spread(rows):
    other = lax.ppermute(rows, "dp", CHIP)
    near = lax.ppermute(rows, "dp", CORE)
    far = lax.ppermute(other, "dp", CORE)
    return jnp.concatenate([rows, other, near, far], axis=1)


def collect(kept, sent):
    count = kept.shape[1] // 2
    near = lax.ppermute(sent, "dp", CORE)
    total = kept + near.astype(jnp.float32)
    other = lax.ppermute(total[:, count:].astype(jnp.bfloat16), "dp", CHIP)
    return (total[:, :count] + other.astype(jnp.float32)).astype(jnp.bfloat16)


def dot(spec, left, right):
    return jnp.einsum(spec, left, right, preferred_element_type=jnp.float32)


def body(tokens, router, w_in, w_out, d_out):
    images = tokens.shape[0]
    score_scale = 1.0 / math.sqrt(tokens.shape[2])
    router_full = gather_router(router)
    logits = dot("imd,nd->imn", tokens, router_full) * score_scale
    combine = jax.nn.softmax(logits, axis=2)
    dispatch = jax.nn.softmax(logits, axis=1)
    dispatch_rounded = dispatch.astype(jnp.bfloat16)
    combine_rounded = combine.astype(jnp.bfloat16)
    slot_part = dot("imn,imd->ind", dispatch_rounded, tokens).astype(jnp.bfloat16)
    grad_part = dot("imn,imd->ind", combine_rounded, d_out).astype(jnp.bfloat16)
    slots = spread(send_in(slot_part))
    slot_grads = spread(send_in(grad_part))
    half = slots.shape[1] // 2

    before = dot("erd,edf->erf", slots, w_in)
    below = 0.5 * (1.0 + lax.erf(before * math.sqrt(0.5)))
    slope = below + before * (jnp.exp(-0.5 * before * before) * (1.0 / math.sqrt(2.0 * math.pi)))
    active = (before * below).astype(jnp.bfloat16)
    out_sent = dot("erf,efd->erd", active[:, half:], w_out).astype(jnp.bfloat16)
    out_kept = dot("erf,efd->erd", active[:, :half], w_out)
    expert_out = send_out(collect(out_kept, out_sent), images)

    grad_before = (dot("erd,efd->erf", slot_grads, w_out) * slope).astype(jnp.bfloat16)
    back_sent = dot("erf,edf->erd", grad_before[:, half:], w_in).astype(jnp.bfloat16)
    back_kept = dot("erf,edf->erd", grad_before[:, :half], w_in)
    slot_back = send_out(collect(back_kept, back_sent), images)
    d_w_out = dot("erf,erd->efd", active, slot_grads).astype(jnp.bfloat16)

    grad_combine = dot("imd,ind->imn", d_out, expert_out)
    combine_part = combine * (grad_combine - jnp.sum(combine * grad_combine, axis=2, keepdims=True))
    grad_dispatch = dot("imd,ind->imn", tokens, slot_back)
    dispatch_part = dispatch * (
        grad_dispatch - jnp.sum(dispatch * grad_dispatch, axis=1, keepdims=True)
    )
    logit_grad = ((combine_part + dispatch_part) * score_scale).astype(jnp.bfloat16)
    router_term = dot("imn,imd->nd", logit_grad, tokens)
    d_router = reduce_router(router_term)
    d_tokens = (
        dot("imn,ind->imd", dispatch_rounded, slot_back) + dot("imn,nd->imd", logit_grad, router_full)
    ).astype(jnp.bfloat16)
    return (d_tokens, d_router, d_w_out)


def solution(mesh):
    placed = (
        P(ALL, None, None),
        P(ALL, None),
        P("expert", None, "dp"),
        P("expert", "dp", None),
        P(ALL, None, None),
    )
    return jax.shard_map(
        body,
        mesh=mesh,
        in_specs=placed,
        out_specs=(P(ALL, None, None), P(ALL, None), P("expert", "dp", None)),
        check_vma=False,
    )
```

```python
import functools
import math

import jax
import jax.numpy as jnp
from jax import lax
from jax.experimental import pallas as pl
from jax.experimental.pallas import tpu as pltpu
from jax.sharding import PartitionSpec as P

ALL = ("zl", "core", "xy", "zh")
PLANE = ("core", "xy")
SWAP = [(0, 1), (1, 0)]
CROSS = [(index, index ^ 3) for index in range(4)]
MIB = 2**20
FREE = pl.CostEstimate(flops=0, bytes_accessed=0, transcendentals=0)


def gather_router(router):
    rows = lax.axis_size(ALL) * router.shape[0]
    spread = jnp.broadcast_to(router.reshape(1, 10, 128), (rows, 10, 128))
    return lax.all_to_all(spread, ALL, split_axis=0, concat_axis=0, tiled=True).reshape(rows, -1)


def reduce_router(router_term):
    received = lax.all_to_all(router_term, ALL, split_axis=0, concat_axis=0, tiled=True)
    return jnp.sum(received.astype(jnp.float32), axis=0).reshape(1, -1)


def exchange(blocks):
    return lax.all_to_all(blocks, PLANE, split_axis=0, concat_axis=0, tiled=True)


def after(first, *later):
    return lax.optimization_barrier((first,) + later)[1:]


def product(left, right, left_dim=1, right_dim=0):
    dims = (((left_dim,), (right_dim,)), ((), ()))
    return lax.dot_general(left, right, dims, preferred_element_type=jnp.float32)


def moved(source_of, rows):
    count = rows.shape[0]
    source = source_of(lax.broadcasted_iota(jnp.int32, (count, count), 0))
    column = lax.broadcasted_iota(jnp.int32, (count, count), 1)
    pick = jnp.where(source == column, 1.0, 0.0).astype(rows.dtype)
    return product(pick, rows).astype(rows.dtype)


def bits(number, *widths):
    fields = []
    for width in reversed(widths):
        fields.append(number & ((1 << width) - 1))
        number = number >> width
    return fields[::-1]


def wire_from_slots(high, row):
    core, place, tensor, half, image, expert = bits(row, 1, 4, 1, 1, 1, 1)
    return (tensor << 8) | (image << 7) | (place << 3) | ((half ^ high) << 2) | (core << 1) | expert


def sorted_from_wire(row):
    expert, half, tensor, core, place, image = bits(row, 1, 1, 1, 1, 4, 1)
    return (core << 8) | (place << 4) | (tensor << 3) | (half << 2) | (image << 1) | expert


def wire_from_sorted(row):
    core, place, tensor, half, image, expert = bits(row, 1, 4, 1, 1, 1, 1)
    return (expert << 8) | (half << 7) | (tensor << 6) | (core << 5) | (place << 1) | image


def slots_from_wire(high, row):
    tensor, image, place, here, core, expert = bits(row, 1, 1, 4, 1, 1, 1)
    return (core << 8) | (place << 4) | (tensor << 3) | ((here ^ high) << 2) | (image << 1) | expert


def call(kernel, outs, arrays, scalars=(), limit=20, specs=None, out_specs=None, **more):
    whole = [pl.BlockSpec(memory_space=pltpu.VMEM)] * len(arrays)
    return pl.pallas_call(
        kernel,
        in_specs=[pl.BlockSpec(memory_space=pltpu.SMEM)] * len(scalars) + (specs or whole),
        out_specs=out_specs or [pl.BlockSpec(memory_space=pltpu.VMEM)] * len(outs),
        out_shape=[jax.ShapeDtypeStruct(*out) for out in outs],
        compiler_params=pltpu.CompilerParams(vmem_limit_bytes=limit * MIB),
        cost_estimate=FREE,
        **more,
    )(*scalars, *arrays)


def front_kernel(score_scale, high, tokens, router, d_out, wire, dispatch, combine):
    slots, grads = [], []
    for image in range(2):
        logits = product(tokens[image], router[...], 1, 1) * score_scale
        raised = jnp.exp(logits - jnp.max(logits, axis=0, keepdims=True))
        spread = raised / jnp.sum(raised, axis=0, keepdims=True)
        dispatch[image] = spread
        slots.append(product(spread.astype(wire.dtype), tokens[image], 0, 0).astype(wire.dtype))
        raised = jnp.exp(logits - jnp.max(logits, axis=1, keepdims=True))
        spread = raised / jnp.sum(raised, axis=1, keepdims=True)
        combine[image] = spread
        grads.append(product(spread.astype(wire.dtype), d_out[image], 0, 0).astype(wire.dtype))
    rows = jnp.concatenate(slots + grads, axis=0)
    wire[...] = moved(functools.partial(wire_from_slots, high[0]), rows).reshape(wire.shape)


def sort_kernel(wire, *parts):
    rows = moved(sorted_from_wire, wire[...].reshape(512, -1))
    for index, part in enumerate(parts):
        part[...] = rows[128 * index : 128 * index + 128].reshape(part.shape)


def spread(own, other):
    cross = lax.ppermute(other, ("zl", "zh"), CROSS)
    pair = lax.ppermute(own, "zl", SWAP)
    return [own, pair, cross, lax.ppermute(cross, "zl", SWAP)]


def expert_kernel(chunk, core, *refs):
    blocks, weights, refs = refs[:4], refs[4:8], refs[8:]
    parts, (active, grads), (held_in, held_out, sems) = refs[:4], refs[4:6], refs[6:]
    expert = 2 * core[0] + chunk
    copies = []
    for index, weight in enumerate(weights):
        held = (held_in if index % 2 == 0 else held_out).at[index // 2]
        copies.append(pltpu.make_async_copy(weight.at[expert], held, sems.at[index]))
    for copy in copies:
        copy.start()
    rows = jnp.concatenate([block[0] for block in blocks], axis=0)
    grad = jnp.concatenate([block[1] for block in blocks], axis=0)
    grads[...] = grad
    out = back = None
    for quarter in range(2):
        copies[2 * quarter].wait()
        before = product(rows, held_in[quarter])
        below = 0.5 + 0.5 * lax.erf(before * math.sqrt(0.5))
        bell = jnp.exp(-0.5 * before * before) * (1.0 / math.sqrt(2.0 * math.pi))
        slope = below + before * bell
        rounded = (before * below).astype(active.dtype)
        active[quarter] = rounded
        copies[2 * quarter + 1].wait()
        part = product(rounded, held_out[quarter])
        out = part if out is None else out + part
        rounded = (product(grad, held_out[quarter], 1, 1) * slope).astype(grad.dtype)
        part = product(rounded, held_in[quarter], 1, 1)
        back = part if back is None else back + part
    for index, part in enumerate(parts):
        mine = slice(64 * index, 64 * index + 64)
        part[0] = out[mine].astype(part.dtype)
        part[1] = back[mine].astype(part.dtype)


def expert_call(chunk, core, blocks, weights):
    half = jnp.bfloat16
    _, width, hidden = weights[0].shape
    vmem = pl.BlockSpec(memory_space=pltpu.VMEM)
    outs = [((2, 64, width), half)] * 4 + [((2, 256, hidden), half), ((256, width), half)]
    return call(
        functools.partial(expert_kernel, chunk),
        outs,
        list(blocks) + list(weights),
        [core],
        limit=56,
        specs=[vmem] * 4 + [pl.BlockSpec(memory_space=pltpu.HBM)] * 4,
        scratch_shapes=[
            pltpu.VMEM((2, width, hidden), half),
            pltpu.VMEM((2, hidden, width), half),
            pltpu.SemaphoreType.DMA((4,)),
        ],
    )


def sum_kernel(left, right, total):
    total[...] = (left[...].astype(jnp.float32) + right[...].astype(jnp.float32)).astype(total.dtype)


def sum_of(left, right):
    return call(sum_kernel, [(left.shape, left.dtype)], [left, right])[0]


def unsort_kernel(*refs):
    wire = refs[6]
    rows = []
    for index in range(2):
        own, pair, other = refs[3 * index : 3 * index + 3]
        total = own[...].astype(jnp.float32) + pair[...].astype(jnp.float32)
        rows += [total.astype(wire.dtype).reshape(128, -1), other[...].reshape(128, -1)]
    wire[...] = moved(wire_from_sorted, jnp.concatenate(rows, axis=0)).reshape(wire.shape)


def score_kernel(score_scale, high, wire, tokens, d_out, dispatch, combine, logit_grad, slot_back, term):
    rows = moved(functools.partial(slots_from_wire, high[0]), wire[...].reshape(512, -1))
    expert_out, back = rows[:256], rows[256:]
    slot_back[...] = back
    total = None
    for image in range(2):
        mine = slice(128 * image, 128 * image + 128)
        grad = product(d_out[image], expert_out[mine], 1, 1)
        share = combine[image]
        score = share * (grad - jnp.sum(share * grad, axis=1, keepdims=True))
        grad = product(tokens[image], back[mine], 1, 1)
        share = dispatch[image]
        score = score + share * (grad - jnp.sum(share * grad, axis=0, keepdims=True))
        score = (score * score_scale).astype(logit_grad.dtype)
        logit_grad[image] = score
        part = product(score, tokens[image], 0, 0)
        total = part if total is None else total + part
    for index in range(term.shape[1]):
        term[:, index] = total[:, 128 * index : 128 * index + 128].astype(term.dtype)


def token_kernel(dispatch, logit_grad, slot_back, router, d_tokens):
    for image in range(2):
        mine = slice(128 * image, 128 * image + 128)
        total = product(dispatch[image].astype(slot_back.dtype), slot_back[mine])
        d_tokens[image] = (total + product(logit_grad[image], router[...])).astype(d_tokens.dtype)


def weight_kernel(active, grads, mine, away):
    mine[...] = product(active[0], grads[...], 0, 0).astype(mine.dtype)
    away[...] = product(active[1], grads[...], 0, 0).astype(away.dtype)


def gather_kernel(core, *refs):
    blocks, whole = refs[:4], refs[4]
    step = pl.program_id(0)
    source = step ^ (2 * core[0])
    for index, block in enumerate(blocks):

        @pl.when(source == index)
        def _():
            whole[0] = block[...]


def body(tokens, router, w_in, w_out, d_out):
    images, count, width = tokens.shape
    slots = 128
    _, _, hidden = w_in.shape
    score_scale = 1.0 / math.sqrt(width)
    half = jnp.bfloat16
    high = lax.axis_index("zh").reshape(1).astype(jnp.int32)
    core = lax.axis_index("core").reshape(1).astype(jnp.int32)
    far_in = lax.ppermute(w_in, "core", SWAP)
    far_out = lax.ppermute(w_out, "core", SWAP)
    router_full = gather_router(router)
    weights = ((images, count, slots), jnp.float32)
    wire, dispatch, combine = call(
        functools.partial(front_kernel, score_scale),
        [((32, 16, width), half), weights, weights],
        [tokens, router_full, d_out],
        [high],
    )
    (wire,) = after(far_out, *after(far_in, exchange(wire)))
    own_0, other_0, own_1, other_1 = call(sort_kernel, [((2, 64, width), half)] * 4, [wire])
    rows_0 = spread(own_0, other_0)
    rows_1 = spread(own_1, other_1)
    shards = [w_in, w_out, far_in, far_out]

    rows_0 = after(rows_1[2], *rows_0)
    *parts_0, active_0, grads_0 = expert_call(0, core, rows_0, shards)
    rows_1[1:] = after(parts_0[0], *rows_1[1:])
    *parts_1, active_1, grads_1 = expert_call(1, core, rows_1, shards)
    far_0 = lax.ppermute(parts_0[3], "zl", SWAP)
    pair_0 = lax.ppermute(parts_0[1], "zl", SWAP)
    far_1 = lax.ppermute(parts_1[3], "zl", SWAP)
    pair_1 = lax.ppermute(parts_1[1], "zl", SWAP)
    far_0, pair_0 = after(parts_1[0], far_0, pair_0)
    cross_0 = sum_of(parts_0[2], far_0)
    other_0 = lax.ppermute(cross_0, ("zl", "zh"), CROSS)
    (far_1,) = after(cross_0, far_1)
    cross_1 = sum_of(parts_1[2], far_1)
    other_1 = lax.ppermute(cross_1, ("zl", "zh"), CROSS)
    shape = [((hidden, width), half)] * 2
    mine_0, away_0 = call(weight_kernel, shape, [active_0, grads_0])
    mine_1, away_1 = call(weight_kernel, shape, [active_1, grads_1])
    wire = call(
        unsort_kernel,
        [((32, 16, width), half)],
        [parts_0[0], pair_0, other_0, parts_1[0], pair_1, other_1],
    )[0]
    wire = exchange(wire)
    came_0 = lax.ppermute(away_0, "core", SWAP)
    came_1 = lax.ppermute(away_1, "core", SWAP)

    logit_grad, slot_back, term = call(
        functools.partial(score_kernel, score_scale),
        [((images, count, slots), half), ((images * slots, width), half), ((slots, width // 128, 128), half)],
        [wire, tokens, d_out, dispatch, combine],
        [high],
    )
    d_router = reduce_router(term)
    d_tokens = call(
        token_kernel,
        [((images, count, width), half)],
        [dispatch, logit_grad, slot_back, router_full],
    )[0]
    came_0, came_1 = after(logit_grad, came_0, came_1)
    d_w_out = call(
        gather_kernel,
        [(w_out.shape, half)],
        [mine_0, mine_1, came_0, came_1],
        [core],
        out_specs=[pl.BlockSpec((1, hidden, width), lambda step: (step, 0, 0))],
        grid=(4,),
    )[0]
    return (d_tokens, d_router, d_w_out)


def solution(mesh):
    split = jax.sharding.Mesh(mesh.devices.reshape(2, 2, 16, 2), ALL)
    dp, expert = ("zl", "core"), ("xy", "zh")
    placed = (
        P(ALL, None, None),
        P(ALL, None),
        P(expert, None, dp),
        P(expert, dp, None),
        P(ALL, None, None),
    )
    return jax.shard_map(
        body,
        mesh=split,
        in_specs=placed,
        out_specs=(P(ALL, None, None), P(ALL, None), P(expert, dp, None)),
        check_vma=False,
    )
```

```python
import functools
import math

import jax
import jax.numpy as jnp
from jax import lax
from jax.experimental import pallas as pl
from jax.experimental.pallas import tpu as pltpu
from jax.sharding import PartitionSpec as P

ALL = ("zl", "core", "xy", "zh")
PLANE = ("core", "xy")
SWAP = [(0, 1), (1, 0)]
CROSS = [(index, index ^ 3) for index in range(4)]
MIB = 2**20
FREE = pl.CostEstimate(flops=0, bytes_accessed=0, transcendentals=0)


def gather_router(router):
    rows = lax.axis_size(ALL) * router.shape[0]
    spread = jnp.broadcast_to(router.reshape(1, 10, 128), (rows, 10, 128))
    return lax.all_to_all(spread, ALL, split_axis=0, concat_axis=0, tiled=True).reshape(rows, -1)


def exchange(blocks):
    return lax.all_to_all(blocks, PLANE, split_axis=0, concat_axis=0, tiled=True)


def after(first, *later):
    return lax.optimization_barrier((first,) + later)[1:]


def product(left, right, left_dim=1, right_dim=0):
    dims = (((left_dim,), (right_dim,)), ((), ()))
    return lax.dot_general(left, right, dims, preferred_element_type=jnp.float32)


def moved(source_of, rows):
    count = rows.shape[0]
    source = source_of(lax.broadcasted_iota(jnp.int32, (count, count), 0))
    column = lax.broadcasted_iota(jnp.int32, (count, count), 1)
    pick = jnp.where(source == column, 1.0, 0.0).astype(rows.dtype)
    return product(pick, rows)


def bits(number, *widths):
    fields = []
    for width in reversed(widths):
        fields.append(number & ((1 << width) - 1))
        number = number >> width
    return fields[::-1]


def wire_from_slots(high, row):
    core, place, half, image, expert = bits(row, 1, 4, 1, 1, 1)
    return (image << 7) | (place << 3) | ((half ^ high) << 2) | (core << 1) | expert


def sorted_from_wire(row):
    expert, half, tensor, place, image = bits(row, 1, 1, 1, 4, 1)
    return (place << 4) | (tensor << 3) | (half << 2) | (image << 1) | expert


def wire_from_sorted(row):
    place, tensor, half, image, expert = bits(row, 4, 1, 1, 1, 1)
    return (expert << 7) | (half << 6) | (tensor << 5) | (place << 1) | image


def slots_from_wire(high, row):
    tensor, image, place, here, core, expert = bits(row, 1, 1, 4, 1, 1, 1)
    return (core << 8) | (place << 4) | (tensor << 3) | ((here ^ high) << 2) | (image << 1) | expert


def call(
    kernel, outs, arrays, scalars=(), limit=20, specs=None, out_specs=None, cost=FREE, **more
):
    whole = [pl.BlockSpec(memory_space=pltpu.VMEM)] * len(arrays)
    return pl.pallas_call(
        kernel,
        in_specs=[pl.BlockSpec(memory_space=pltpu.SMEM)] * len(scalars) + (specs or whole),
        out_specs=out_specs or [pl.BlockSpec(memory_space=pltpu.VMEM)] * len(outs),
        out_shape=[(out[2] if len(out) > 2 else jax.ShapeDtypeStruct)(*out[:2]) for out in outs],
        compiler_params=pltpu.CompilerParams(vmem_limit_bytes=limit * MIB),
        cost_estimate=cost,
        **more,
    )(*scalars, *arrays)


def front_kernel(
    score_scale, high, tokens, router, d_out, wire, dispatch, combine, held_0, held_1, sems
):
    slots, grads = [], []
    for image in range(2):
        logits = product(tokens[image], router[...], 1, 1) * score_scale
        raised = jnp.exp(logits - jnp.max(logits, axis=0, keepdims=True))
        share = raised / jnp.sum(raised, axis=0, keepdims=True)
        held_0[image] = share
        slots.append(product(share.astype(wire.dtype), tokens[image], 0, 0).astype(wire.dtype))
        raised = jnp.exp(logits - jnp.max(logits, axis=1, keepdims=True))
        share = raised / jnp.sum(raised, axis=1, keepdims=True)
        held_1[image] = share
        grads.append(product(share.astype(wire.dtype), d_out[image], 0, 0).astype(wire.dtype))
    copies = [
        pltpu.make_async_copy(held_0, dispatch, sems.at[0]),
        pltpu.make_async_copy(held_1, combine, sems.at[1]),
    ]
    for copy in copies:
        copy.start()
    order = functools.partial(wire_from_slots, high[0])
    rows = [moved(order, jnp.concatenate(part, axis=0)) for part in (slots, grads)]
    rows = jnp.concatenate([part.reshape(32, 8, -1) for part in rows], axis=1)
    wire[...] = rows.astype(wire.dtype)
    for copy in copies:
        copy.wait()


def sort_kernel(wire, *parts):
    for core in range(2):
        rows = wire[16 * core : 16 * core + 16].reshape(256, -1)
        rows = moved(sorted_from_wire, rows).astype(wire.dtype)
        for index in range(8):
            part = parts[index // 2]
            part[index % 2, 32 * core : 32 * core + 32] = rows[32 * index : 32 * index + 32]


def expert_kernel(chunk, core, *refs):
    blocks, weights, refs = refs[:4], refs[4:8], refs[8:]
    parts, (active, grads), (held_in, held_out, sems) = refs[:4], refs[4:6], refs[6:]
    expert = 2 * core[0] + chunk
    copies = []
    for index, weight in enumerate(weights):
        held = (held_in if index % 2 == 0 else held_out).at[index // 2]
        copies.append(pltpu.make_async_copy(weight.at[expert], held, sems.at[index]))
    for copy in copies:
        copy.start()
    rows = jnp.concatenate([block[0] for block in blocks], axis=0)
    grad = jnp.concatenate([block[1] for block in blocks], axis=0)
    grads[...] = grad
    out = back = None
    for quarter in range(2):
        copies[2 * quarter].wait()
        before = product(rows, held_in[quarter])
        below = 0.5 + 0.5 * lax.erf(before * math.sqrt(0.5))
        bell = jnp.exp(-0.5 * before * before) * (1.0 / math.sqrt(2.0 * math.pi))
        slope = below + before * bell
        rounded = (before * below).astype(active.dtype)
        active[quarter] = rounded
        copies[2 * quarter + 1].wait()
        part = product(rounded, held_out[quarter])
        out = part if out is None else out + part
        rounded = (product(grad, held_out[quarter], 1, 1) * slope).astype(grad.dtype)
        part = product(rounded, held_in[quarter], 1, 1)
        back = part if back is None else back + part
    for index, part in enumerate(parts):
        mine = slice(64 * index, 64 * index + 64)
        part[0] = out[mine].astype(part.dtype)
        part[1] = back[mine].astype(part.dtype)


def expert_call(chunk, core, blocks, weights):
    half = jnp.bfloat16
    _, width, hidden = weights[0].shape
    vmem = pl.BlockSpec(memory_space=pltpu.VMEM)
    outs = [((2, 64, width), half)] * 4 + [((2, 256, hidden), half), ((256, width), half)]
    return call(
        functools.partial(expert_kernel, chunk),
        outs,
        list(blocks) + list(weights),
        [core],
        limit=28,
        specs=[vmem] * 4 + [pl.BlockSpec(memory_space=pltpu.HBM)] * 4,
        cost=pl.CostEstimate(flops=8 * 10**9, bytes_accessed=24 * MIB, transcendentals=0),
        scratch_shapes=[
            pltpu.VMEM((2, width, hidden), half),
            pltpu.VMEM((2, hidden, width), half),
            pltpu.SemaphoreType.DMA((4,)),
        ],
    )


def sum_kernel(left, right, total):
    total[...] = (left[...].astype(jnp.float32) + right[...].astype(jnp.float32)).astype(total.dtype)


def sum_of(left, right):
    return call(sum_kernel, [(left.shape, left.dtype)], [left, right])[0]


def unsort_kernel(*refs):
    wire = refs[6]
    totals = []
    for index in range(2):
        own, pair, other = refs[3 * index : 3 * index + 3]
        total = own[...].astype(jnp.float32) + pair[...].astype(jnp.float32)
        totals += [total.astype(wire.dtype), other[...]]
    for core in range(2):
        mine = slice(32 * core, 32 * core + 32)
        rows = [total[tensor, mine] for total in totals for tensor in range(2)]
        rows = moved(wire_from_sorted, jnp.concatenate(rows, axis=0)).astype(wire.dtype)
        wire[16 * core : 16 * core + 16] = rows.reshape(16, 16, -1)


def score_kernel(
    score_scale, high, wire, tokens, d_out, dispatch, combine,
    logit_grad, slot_back, term, held_back, held_term, sems,
):
    rows = moved(functools.partial(slots_from_wire, high[0]), wire[...].reshape(512, -1))
    rows = rows.astype(wire.dtype)
    expert_out, back = rows[:256], rows[256:]
    held_back[...] = back
    copies = [
        pltpu.make_async_copy(held_back, slot_back, sems.at[0]),
        pltpu.make_async_copy(held_term, term, sems.at[1]),
    ]
    copies[0].start()
    total = None
    for image in range(2):
        mine = slice(128 * image, 128 * image + 128)
        grad = product(d_out[image], expert_out[mine], 1, 1)
        share = combine[image]
        score = share * (grad - jnp.sum(share * grad, axis=1, keepdims=True))
        grad = product(tokens[image], back[mine], 1, 1)
        share = dispatch[image]
        score = score + share * (grad - jnp.sum(share * grad, axis=0, keepdims=True))
        score = (score * score_scale).astype(logit_grad.dtype)
        logit_grad[image] = score
        part = product(score, tokens[image], 0, 0)
        total = part if total is None else total + part
    for index in range(term.shape[1]):
        held_term[:, index] = total[:, 128 * index : 128 * index + 128].astype(term.dtype)
    copies[1].start()
    for copy in copies:
        copy.wait()


def token_kernel(dispatch, logit_grad, slot_back, router, d_tokens):
    for image in range(2):
        mine = slice(128 * image, 128 * image + 128)
        total = product(dispatch[image].astype(slot_back.dtype), slot_back[mine])
        d_tokens[image] = (total + product(logit_grad[image], router[...])).astype(d_tokens.dtype)


def weight_kernel(chunk, core, active, grads, *refs):
    whole, away, held, sems = refs[-4:]
    copies = []
    for index, ref in enumerate((whole.at[2 * core[0] + chunk], away)):
        held[index] = product(active[index], grads[...], 0, 0).astype(held.dtype)
        copies.append(pltpu.make_async_copy(held.at[index], ref, sems.at[index]))
        copies[index].start()
    for copy in copies:
        copy.wait()


def weight_call(chunk, core, active, grads, *whole):
    shape = (active.shape[2], grads.shape[1])
    hbm = pl.BlockSpec(memory_space=pltpu.HBM)
    return call(
        functools.partial(weight_kernel, chunk),
        [((4,) + shape, grads.dtype, pltpu.HBM), (shape, grads.dtype, pltpu.HBM)],
        [active, grads, *whole],
        [core],
        specs=[pl.BlockSpec(memory_space=pltpu.VMEM)] * 2 + [hbm] * len(whole),
        out_specs=[hbm] * 2,
        scratch_shapes=[pltpu.VMEM((2,) + shape, grads.dtype), pltpu.SemaphoreType.DMA((2,))],
        input_output_aliases={3: 0} if whole else {},
    )


def gather_kernel(core, came_0, came_1, _, whole, held, sems):
    first = 2 - 2 * core[0]
    arrive = [
        pltpu.make_async_copy(came, held.at[index], sems.at[index])
        for index, came in enumerate((came_0, came_1))
    ]
    leave = [
        pltpu.make_async_copy(held.at[index], whole.at[first + index], sems.at[2 + index])
        for index in range(2)
    ]
    for copy in arrive:
        copy.start()
    for coming, going in zip(arrive, leave):
        coming.wait()
        going.start()
    for copy in leave:
        copy.wait()


def gather_call(core, came_0, came_1, whole):
    hbm = pl.BlockSpec(memory_space=pltpu.HBM)
    came = [pltpu.with_memory_space_constraint(part, pltpu.HBM) for part in (came_0, came_1)]
    return call(
        gather_kernel,
        [(whole.shape, whole.dtype, pltpu.HBM)],
        [*came, whole],
        [core],
        specs=[hbm] * 3,
        out_specs=[hbm],
        scratch_shapes=[
            pltpu.VMEM((2,) + whole.shape[1:], whole.dtype),
            pltpu.SemaphoreType.DMA((4,)),
        ],
        input_output_aliases={3: 0},
    )[0]


def body(tokens, router, w_in, w_out, d_out):
    images, count, width = tokens.shape
    slots = 128
    _, _, hidden = w_in.shape
    score_scale = 1.0 / math.sqrt(width)
    half = jnp.bfloat16
    high = lax.axis_index("zh").reshape(1).astype(jnp.int32)
    core = lax.axis_index("core").reshape(1).astype(jnp.int32)
    far_in = lax.ppermute(w_in, "core", SWAP)
    far_out = lax.ppermute(w_out, "core", SWAP)
    router_full = gather_router(router)
    weights = ((images, count, slots), jnp.float32)
    vmem = pl.BlockSpec(memory_space=pltpu.VMEM)
    hbm = pl.BlockSpec(memory_space=pltpu.HBM)
    wire, dispatch, combine = call(
        functools.partial(front_kernel, score_scale),
        [((32, 16, width), half), weights + (pltpu.HBM,), weights + (pltpu.HBM,)],
        [tokens, router_full, d_out],
        [high],
        out_specs=[vmem, hbm, hbm],
        scratch_shapes=[pltpu.VMEM(*weights)] * 2 + [pltpu.SemaphoreType.DMA((2,))],
    )
    (wire,) = after(far_out, *after(far_in, exchange(wire)))
    own_0, other_0, own_1, other_1 = call(
        sort_kernel,
        [((2, 64, width), half)] * 4,
        [wire],
        cost=pl.CostEstimate(flops=10**6, bytes_accessed=40 * MIB, transcendentals=0),
    )
    pair_0 = lax.ppermute(own_0, "zl", SWAP)
    cross_0 = lax.ppermute(other_0, ("zl", "zh"), CROSS)
    (cross_0,) = after(pair_0, cross_0)
    far_0 = lax.ppermute(cross_0, "zl", SWAP)
    (other_1,) = after(cross_0, other_1)
    cross_1 = lax.ppermute(other_1, ("zl", "zh"), CROSS)
    (own_1,) = after(far_0, own_1)
    pair_1 = lax.ppermute(own_1, "zl", SWAP)
    far_1 = lax.ppermute(cross_1, "zl", SWAP)
    rows_0 = [own_0, pair_0, cross_0, far_0]
    rows_1 = [own_1, pair_1, cross_1, far_1]
    shards = [
        pltpu.with_memory_space_constraint(shard, pltpu.HBM)
        for shard in (w_in, w_out, far_in, far_out)
    ]

    *parts_0, active_0, grads_0 = expert_call(0, core, rows_0, shards)
    rows_1[1::2] = after(parts_0[0], *rows_1[1::2])
    *parts_1, active_1, grads_1 = expert_call(1, core, rows_1, shards)
    far_0 = lax.ppermute(parts_0[3], "zl", SWAP)
    pair_0 = lax.ppermute(parts_0[1], "zl", SWAP)
    far_1 = lax.ppermute(parts_1[3], "zl", SWAP)
    pair_1 = lax.ppermute(parts_1[1], "zl", SWAP)
    (far_0,) = after(parts_1[0], far_0)
    cross_0 = sum_of(parts_0[2], far_0)
    other_0 = lax.ppermute(cross_0, ("zl", "zh"), CROSS)
    (active_0,) = after(cross_0, active_0)
    whole, away_0 = weight_call(0, core, active_0, grads_0)
    (far_1,) = after(away_0, far_1)
    cross_1 = sum_of(parts_1[2], far_1)
    other_1 = lax.ppermute(cross_1, ("zl", "zh"), CROSS)
    (active_1,) = after(cross_1, active_1)
    whole, away_1 = weight_call(1, core, active_1, grads_1, whole)
    other_0, other_1 = after(away_1, other_0, other_1)
    came_0 = lax.ppermute(away_0, "core", SWAP)
    came_1 = lax.ppermute(away_1, "core", SWAP)
    wire = call(
        unsort_kernel,
        [((32, 16, width), half)],
        [parts_0[0], pair_0, other_0, parts_1[0], pair_1, other_1],
    )[0]
    wire = exchange(wire)

    logit_grad, slot_back, term = call(
        functools.partial(score_kernel, score_scale),
        [
            ((images, count, slots), half),
            ((images * slots, width), half, pltpu.HBM),
            ((slots, width // 128, 128), half, pltpu.HBM),
        ],
        [wire, tokens, d_out, dispatch, combine],
        [high],
        out_specs=[vmem, hbm, hbm],
        scratch_shapes=[
            pltpu.VMEM((images * slots, width), half),
            pltpu.VMEM((slots, width // 128, 128), half),
            pltpu.SemaphoreType.DMA((2,)),
        ],
    )
    received = lax.all_to_all(term, ALL, split_axis=0, concat_axis=0, tiled=True)
    d_router = jnp.sum(received.astype(jnp.float32), axis=0).reshape(1, -1)
    d_w_out = gather_call(core, *after(logit_grad, came_0, came_1), whole)
    (slot_back,) = after(d_w_out, slot_back)
    d_tokens = call(
        token_kernel,
        [((images, count, width), half)],
        [dispatch, logit_grad, slot_back, router_full],
    )[0]
    return (d_tokens, d_router, d_w_out)


def solution(mesh):
    split = jax.sharding.Mesh(mesh.devices.reshape(2, 2, 16, 2), ALL)
    dp, expert = ("zl", "core"), ("xy", "zh")
    placed = (
        P(ALL, None, None),
        P(ALL, None),
        P(expert, None, dp),
        P(expert, dp, None),
        P(ALL, None, None),
    )
    return jax.shard_map(
        body,
        mesh=split,
        in_specs=placed,
        out_specs=(P(ALL, None, None), P(ALL, None), P(expert, dp, None)),
        check_vma=False,
    )
```

```python
import functools
import math

import jax
import jax.numpy as jnp
from jax import lax
from jax.experimental import pallas as pl
from jax.experimental.pallas import tpu as pltpu
from jax.sharding import PartitionSpec as P

ALL = ("zl", "core", "xy", "zh")
PLANE = ("core", "xy")
SWAP = [(0, 1), (1, 0)]
CROSS = [(index, index ^ 3) for index in range(4)]
MIB = 2**20
FREE = pl.CostEstimate(flops=0, bytes_accessed=0, transcendentals=0)


def gather_router(router):
    rows = lax.axis_size(ALL) * router.shape[0]
    spread = jnp.broadcast_to(router.reshape(1, 10, 128), (rows, 10, 128))
    return lax.all_to_all(spread, ALL, split_axis=0, concat_axis=0, tiled=True).reshape(rows, -1)


def exchange(blocks):
    return lax.all_to_all(blocks, PLANE, split_axis=0, concat_axis=0, tiled=True)


def after(first, *later):
    return lax.optimization_barrier((first,) + later)[1:]


def product(left, right, left_dim=1, right_dim=0):
    dims = (((left_dim,), (right_dim,)), ((), ()))
    return lax.dot_general(left, right, dims, preferred_element_type=jnp.float32)


def moved(source_of, rows):
    count = rows.shape[0]
    source = source_of(lax.broadcasted_iota(jnp.int32, (count, count), 0))
    column = lax.broadcasted_iota(jnp.int32, (count, count), 1)
    pick = jnp.where(source == column, 1.0, 0.0).astype(rows.dtype)
    return product(pick, rows)


def bits(number, *widths):
    fields = []
    for width in reversed(widths):
        fields.append(number & ((1 << width) - 1))
        number = number >> width
    return fields[::-1]


def wire_from_slots(high, row):
    core, place, half, image, expert = bits(row, 1, 4, 1, 1, 1)
    return (image << 7) | (place << 3) | ((half ^ high) << 2) | (core << 1) | expert


def sorted_from_wire(row):
    expert, half, tensor, place, image = bits(row, 1, 1, 1, 4, 1)
    return (place << 4) | (tensor << 3) | (half << 2) | (image << 1) | expert


def wire_from_sorted(row):
    place, tensor, half, image, expert = bits(row, 4, 1, 1, 1, 1)
    return (expert << 7) | (half << 6) | (tensor << 5) | (place << 1) | image


def slots_from_wire(high, row):
    tensor, image, place, here, core, expert = bits(row, 1, 1, 4, 1, 1, 1)
    return (core << 8) | (place << 4) | (tensor << 3) | ((here ^ high) << 2) | (image << 1) | expert


def call(
    kernel, outs, arrays, scalars=(), limit=20, specs=None, out_specs=None, cost=FREE, **more
):
    whole = [pl.BlockSpec(memory_space=pltpu.VMEM)] * len(arrays)
    return pl.pallas_call(
        kernel,
        in_specs=[pl.BlockSpec(memory_space=pltpu.SMEM)] * len(scalars) + (specs or whole),
        out_specs=out_specs or [pl.BlockSpec(memory_space=pltpu.VMEM)] * len(outs),
        out_shape=[(out[2] if len(out) > 2 else jax.ShapeDtypeStruct)(*out[:2]) for out in outs],
        compiler_params=pltpu.CompilerParams(vmem_limit_bytes=limit * MIB),
        cost_estimate=cost,
        **more,
    )(*scalars, *arrays)


def front_kernel(
    score_scale, high, tokens, router, d_out, wire, dispatch, combine, held_0, held_1, sems
):
    slots, grads = [], []
    for image in range(2):
        logits = product(tokens[image], router[...], 1, 1) * score_scale
        raised = jnp.exp(logits - jnp.max(logits, axis=0, keepdims=True))
        share = raised / jnp.sum(raised, axis=0, keepdims=True)
        held_0[image] = share
        slots.append(product(share.astype(wire.dtype), tokens[image], 0, 0).astype(wire.dtype))
        raised = jnp.exp(logits - jnp.max(logits, axis=1, keepdims=True))
        share = raised / jnp.sum(raised, axis=1, keepdims=True)
        held_1[image] = share
        grads.append(product(share.astype(wire.dtype), d_out[image], 0, 0).astype(wire.dtype))
    copies = [
        pltpu.make_async_copy(held_0, dispatch, sems.at[0]),
        pltpu.make_async_copy(held_1, combine, sems.at[1]),
    ]
    for copy in copies:
        copy.start()
    order = functools.partial(wire_from_slots, high[0])
    rows = [moved(order, jnp.concatenate(part, axis=0)) for part in (slots, grads)]
    rows = jnp.concatenate([part.reshape(32, 8, -1) for part in rows], axis=1)
    wire[...] = rows.astype(wire.dtype)
    for copy in copies:
        copy.wait()


def sort_kernel(wire, *parts):
    for core in range(2):
        rows = wire[16 * core : 16 * core + 16].reshape(256, -1)
        rows = moved(sorted_from_wire, rows).astype(wire.dtype)
        for index in range(8):
            part = parts[index // 2]
            part[index % 2, 32 * core : 32 * core + 32] = rows[32 * index : 32 * index + 32]


def stage_kernel(core, near_in, near_out, far_in, far_out, held_in, held_out, sems):
    copies = []
    for index, (weight, held) in enumerate(
        [(near_in, held_in), (near_out, held_out), (far_in, held_in), (far_out, held_out)]
    ):
        source = weight.at[pl.ds(2 * core[0], 2)]
        copies.append(pltpu.make_async_copy(source, held.at[index // 2], sems.at[index]))
    for copy in copies:
        copy.start()
    for copy in copies:
        copy.wait()


def stage(core, near_in, near_out, far_in, far_out):
    shards = [
        pltpu.with_memory_space_constraint(shard, pltpu.HBM)
        for shard in (near_in, near_out, far_in, far_out)
    ]
    shape = lambda shard: ((2, 2) + shard.shape[1:], shard.dtype, pltpu.VMEM)
    return call(
        stage_kernel,
        [shape(near_in), shape(near_out)],
        shards,
        [core],
        specs=[pl.BlockSpec(memory_space=pltpu.HBM)] * 4,
        scratch_shapes=[pltpu.SemaphoreType.DMA((4,))],
    )


def expert_kernel(chunk, *refs):
    blocks, (held_in, held_out), refs = refs[:4], refs[4:6], refs[6:]
    parts, (active, grads) = refs[:4], refs[4:]
    rows = jnp.concatenate([block[0] for block in blocks], axis=0)
    grad = jnp.concatenate([block[1] for block in blocks], axis=0)
    grads[...] = grad
    out = back = None
    for quarter in range(2):
        first, second = held_in[quarter, chunk], held_out[quarter, chunk]
        before = product(rows, first)
        below = 0.5 + 0.5 * lax.erf(before * math.sqrt(0.5))
        bell = jnp.exp(-0.5 * before * before) * (1.0 / math.sqrt(2.0 * math.pi))
        slope = below + before * bell
        rounded = (before * below).astype(active.dtype)
        active[quarter] = rounded
        part = product(rounded, second)
        out = part if out is None else out + part
        rounded = (product(grad, second, 1, 1) * slope).astype(grad.dtype)
        part = product(rounded, first, 1, 1)
        back = part if back is None else back + part
    for index, part in enumerate(parts):
        mine = slice(64 * index, 64 * index + 64)
        part[0] = out[mine].astype(part.dtype)
        part[1] = back[mine].astype(part.dtype)


def expert_call(chunk, blocks, held):
    half = jnp.bfloat16
    width, hidden = held[0].shape[2:]
    outs = [((2, 64, width), half, pltpu.VMEM)] * 4
    outs += [((2, 256, hidden), half), ((256, width), half)]
    held = [pltpu.with_memory_space_constraint(weight, pltpu.VMEM) for weight in held]
    return call(
        functools.partial(expert_kernel, chunk),
        outs,
        list(blocks) + held,
        cost=pl.CostEstimate(flops=8 * 10**9, bytes_accessed=24 * MIB, transcendentals=0),
    )


def sum_kernel(left, right, total):
    total[...] = (left[...].astype(jnp.float32) + right[...].astype(jnp.float32)).astype(total.dtype)


def sum_of(left, right):
    return call(sum_kernel, [(left.shape, left.dtype)], [left, right])[0]


def unsort_kernel(*refs):
    wire = refs[6]
    totals = []
    for index in range(2):
        own, pair, other = refs[3 * index : 3 * index + 3]
        total = own[...].astype(jnp.float32) + pair[...].astype(jnp.float32)
        totals += [total.astype(wire.dtype), other[...]]
    for core in range(2):
        mine = slice(32 * core, 32 * core + 32)
        rows = [total[tensor, mine] for total in totals for tensor in range(2)]
        rows = moved(wire_from_sorted, jnp.concatenate(rows, axis=0)).astype(wire.dtype)
        wire[16 * core : 16 * core + 16] = rows.reshape(16, 16, -1)


def score_kernel(
    score_scale, high, wire, tokens, d_out, dispatch, combine,
    logit_grad, slot_back, term, held_back, held_term, sems,
):
    rows = moved(functools.partial(slots_from_wire, high[0]), wire[...].reshape(512, -1))
    rows = rows.astype(wire.dtype)
    expert_out, back = rows[:256], rows[256:]
    held_back[...] = back
    copies = [
        pltpu.make_async_copy(held_back, slot_back, sems.at[0]),
        pltpu.make_async_copy(held_term, term, sems.at[1]),
    ]
    copies[0].start()
    total = None
    for image in range(2):
        mine = slice(128 * image, 128 * image + 128)
        grad = product(d_out[image], expert_out[mine], 1, 1)
        share = combine[image]
        score = share * (grad - jnp.sum(share * grad, axis=1, keepdims=True))
        grad = product(tokens[image], back[mine], 1, 1)
        share = dispatch[image]
        score = score + share * (grad - jnp.sum(share * grad, axis=0, keepdims=True))
        score = (score * score_scale).astype(logit_grad.dtype)
        logit_grad[image] = score
        part = product(score, tokens[image], 0, 0)
        total = part if total is None else total + part
    for index in range(term.shape[1]):
        held_term[:, index] = total[:, 128 * index : 128 * index + 128].astype(term.dtype)
    copies[1].start()
    for copy in copies:
        copy.wait()


def token_kernel(dispatch, logit_grad, slot_back, router, d_tokens):
    for image in range(2):
        mine = slice(128 * image, 128 * image + 128)
        total = product(dispatch[image].astype(slot_back.dtype), slot_back[mine])
        d_tokens[image] = (total + product(logit_grad[image], router[...])).astype(d_tokens.dtype)


def weight_kernel(chunk, core, active, grads, *refs):
    whole, away, held, sems = refs[-4:]
    copies = []
    for index, ref in enumerate((whole.at[2 * core[0] + chunk], away)):
        held[index] = product(active[index], grads[...], 0, 0).astype(held.dtype)
        copies.append(pltpu.make_async_copy(held.at[index], ref, sems.at[index]))
        copies[index].start()
    for copy in copies:
        copy.wait()


def weight_call(chunk, core, active, grads, *whole):
    shape = (active.shape[2], grads.shape[1])
    hbm = pl.BlockSpec(memory_space=pltpu.HBM)
    return call(
        functools.partial(weight_kernel, chunk),
        [((4,) + shape, grads.dtype, pltpu.HBM), (shape, grads.dtype, pltpu.HBM)],
        [active, grads, *whole],
        [core],
        specs=[pl.BlockSpec(memory_space=pltpu.VMEM)] * 2 + [hbm] * len(whole),
        out_specs=[hbm] * 2,
        scratch_shapes=[pltpu.VMEM((2,) + shape, grads.dtype), pltpu.SemaphoreType.DMA((2,))],
        input_output_aliases={3: 0} if whole else {},
    )


def gather_kernel(core, came_0, came_1, _, whole, held, sems):
    first = 2 - 2 * core[0]
    arrive = [
        pltpu.make_async_copy(came, held.at[index], sems.at[index])
        for index, came in enumerate((came_0, came_1))
    ]
    leave = [
        pltpu.make_async_copy(held.at[index], whole.at[first + index], sems.at[2 + index])
        for index in range(2)
    ]
    for copy in arrive:
        copy.start()
    for coming, going in zip(arrive, leave):
        coming.wait()
        going.start()
    for copy in leave:
        copy.wait()


def gather_call(core, came_0, came_1, whole):
    hbm = pl.BlockSpec(memory_space=pltpu.HBM)
    came = [pltpu.with_memory_space_constraint(part, pltpu.HBM) for part in (came_0, came_1)]
    return call(
        gather_kernel,
        [(whole.shape, whole.dtype, pltpu.HBM)],
        [*came, whole],
        [core],
        specs=[hbm] * 3,
        out_specs=[hbm],
        scratch_shapes=[
            pltpu.VMEM((2,) + whole.shape[1:], whole.dtype),
            pltpu.SemaphoreType.DMA((4,)),
        ],
        input_output_aliases={3: 0},
    )[0]


def body(tokens, router, w_in, w_out, d_out):
    images, count, width = tokens.shape
    slots = 128
    _, _, hidden = w_in.shape
    score_scale = 1.0 / math.sqrt(width)
    half = jnp.bfloat16
    high = lax.axis_index("zh").reshape(1).astype(jnp.int32)
    core = lax.axis_index("core").reshape(1).astype(jnp.int32)
    far_in = lax.ppermute(w_in, "core", SWAP)
    far_out = lax.ppermute(w_out, "core", SWAP)
    router_full = gather_router(router)
    weights = ((images, count, slots), jnp.float32)
    vmem = pl.BlockSpec(memory_space=pltpu.VMEM)
    hbm = pl.BlockSpec(memory_space=pltpu.HBM)
    wire, dispatch, combine = call(
        functools.partial(front_kernel, score_scale),
        [((32, 16, width), half), weights + (pltpu.HBM,), weights + (pltpu.HBM,)],
        [tokens, pltpu.with_memory_space_constraint(router_full, pltpu.VMEM), d_out],
        [high],
        out_specs=[vmem, hbm, hbm],
        scratch_shapes=[pltpu.VMEM(*weights)] * 2 + [pltpu.SemaphoreType.DMA((2,))],
    )
    (wire,) = after(far_out, *after(far_in, exchange(wire)))
    own_0, other_0, own_1, other_1 = call(
        sort_kernel,
        [((2, 64, width), half, kind) for kind in (pltpu.HBM, pltpu.VMEM) * 2],
        [wire],
        cost=pl.CostEstimate(flops=10**6, bytes_accessed=40 * MIB, transcendentals=0),
    )
    pair_0, pair_1 = (lax.ppermute(own, "zl", SWAP) for own in (own_0, own_1))
    cross_0 = lax.ppermute(other_0, ("zl", "zh"), CROSS)
    cross_1 = lax.ppermute(other_1, ("zl", "zh"), CROSS)
    held = stage(core, *after(own_0, w_in, w_out, far_in, far_out))
    (cross_0,) = after(held[0], *after(pair_0, cross_0))
    (cross_1,) = after(pair_1, cross_1)
    far_0, far_1 = (lax.ppermute(cross, "zl", SWAP) for cross in (cross_0, cross_1))
    (far_0,) = after(cross_1, far_0)
    rows_0 = [own_0, pair_0, cross_0, far_0]
    rows_1 = [own_1, pair_1, cross_1, far_1]
    *parts_0, active_0, grads_0 = expert_call(0, rows_0, held)
    rows_1[3:] = after(parts_0[0], *rows_1[3:])
    *parts_1, active_1, grads_1 = expert_call(1, rows_1, held)
    far_0 = lax.ppermute(parts_0[3], "zl", SWAP)
    pair_0 = lax.ppermute(parts_0[1], "zl", SWAP)
    far_1 = lax.ppermute(parts_1[3], "zl", SWAP)
    pair_1 = lax.ppermute(parts_1[1], "zl", SWAP)
    (far_0,) = after(parts_1[0], far_0)
    cross_0 = sum_of(parts_0[2], far_0)
    other_0 = lax.ppermute(cross_0, ("zl", "zh"), CROSS)
    (active_0,) = after(cross_0, active_0)
    whole, away_0 = weight_call(0, core, active_0, grads_0)
    (far_1,) = after(away_0, far_1)
    cross_1 = sum_of(parts_1[2], far_1)
    other_1 = lax.ppermute(cross_1, ("zl", "zh"), CROSS)
    (active_1,) = after(pair_0, *after(cross_1, active_1))
    whole, away_1 = weight_call(1, core, active_1, grads_1, whole)
    other_0, other_1 = after(away_1, other_0, other_1)
    (away_0,) = after(away_1, away_0)
    came_0 = lax.ppermute(away_0, "core", SWAP)
    came_1 = lax.ppermute(away_1, "core", SWAP)
    wire = call(
        unsort_kernel,
        [((32, 16, width), half)],
        [parts_0[0], pair_0, other_0, parts_1[0], pair_1, other_1],
    )[0]
    wire = exchange(wire)

    logit_grad, slot_back, term = call(
        functools.partial(score_kernel, score_scale),
        [
            ((images, count, slots), half),
            ((images * slots, width), half, pltpu.HBM),
            ((slots, width // 128, 128), half, pltpu.HBM),
        ],
        [wire, tokens, d_out, dispatch, combine],
        [high],
        out_specs=[vmem, hbm, hbm],
        scratch_shapes=[
            pltpu.VMEM((images * slots, width), half),
            pltpu.VMEM((slots, width // 128, 128), half),
            pltpu.SemaphoreType.DMA((2,)),
        ],
    )
    received = lax.all_to_all(term, ALL, split_axis=0, concat_axis=0, tiled=True)
    d_router = jnp.sum(received.astype(jnp.float32), axis=0).reshape(1, -1)
    d_w_out = gather_call(core, *after(logit_grad, came_0, came_1), whole)
    (slot_back,) = after(d_w_out, slot_back)
    d_tokens = call(
        token_kernel,
        [((images, count, width), half)],
        [dispatch, logit_grad, slot_back, router_full],
    )[0]
    return (d_tokens, d_router, d_w_out)


def solution(mesh):
    split = jax.sharding.Mesh(mesh.devices.reshape(2, 2, 16, 2), ALL)
    dp, expert = ("zl", "core"), ("xy", "zh")
    placed = (
        P(ALL, None, None),
        P(ALL, None),
        P(expert, None, dp),
        P(expert, dp, None),
        P(ALL, None, None),
    )
    return jax.shard_map(
        body,
        mesh=split,
        in_specs=placed,
        out_specs=(P(ALL, None, None), P(ALL, None), P(expert, dp, None)),
        check_vma=False,
    )
```

```python
import functools
import math

import jax
import jax.numpy as jnp
from jax import lax
from jax.experimental import pallas as pl
from jax.experimental.pallas import tpu as pltpu
from jax.sharding import PartitionSpec as P

ALL = ("zl", "core", "xy", "zh")
PLANE = ("core", "xy")
SWAP = [(0, 1), (1, 0)]
CROSS = [(index, index ^ 3) for index in range(4)]
MIB = 2**20
FREE = pl.CostEstimate(flops=0, bytes_accessed=0, transcendentals=0)


def exchange(blocks):
    return lax.all_to_all(blocks, PLANE, split_axis=0, concat_axis=0, tiled=True)


def after(first, *later):
    return lax.optimization_barrier((first,) + later)[1:]


def product(left, right, left_dim=1, right_dim=0):
    dims = (((left_dim,), (right_dim,)), ((), ()))
    return lax.dot_general(left, right, dims, preferred_element_type=jnp.float32)


def moved(source_of, rows):
    count = rows.shape[0]
    source = source_of(lax.broadcasted_iota(jnp.int32, (count, count), 0))
    column = lax.broadcasted_iota(jnp.int32, (count, count), 1)
    pick = jnp.where(source == column, 1.0, 0.0).astype(rows.dtype)
    return product(pick, rows)


def bits(number, *widths):
    fields = []
    for width in reversed(widths):
        fields.append(number & ((1 << width) - 1))
        number = number >> width
    return fields[::-1]


def wire_from_slots(high, row):
    core, place, half, image, expert = bits(row, 1, 4, 1, 1, 1)
    return (image << 7) | (place << 3) | ((half ^ high) << 2) | (core << 1) | expert


def sorted_from_wire(row):
    expert, half, tensor, place, image = bits(row, 1, 1, 1, 4, 1)
    return (place << 4) | (tensor << 3) | (half << 2) | (image << 1) | expert


def wire_from_sorted(row):
    place, tensor, half, image, expert = bits(row, 4, 1, 1, 1, 1)
    return (expert << 7) | (half << 6) | (tensor << 5) | (place << 1) | image


def slots_from_wire(high, row):
    tensor, image, place, here, core, expert = bits(row, 1, 1, 4, 1, 1, 1)
    return (core << 8) | (place << 4) | (tensor << 3) | ((here ^ high) << 2) | (image << 1) | expert


def call(
    kernel, outs, arrays, scalars=(), limit=20, specs=None, out_specs=None, cost=FREE, **more
):
    whole = [pl.BlockSpec(memory_space=pltpu.VMEM)] * len(arrays)
    return pl.pallas_call(
        kernel,
        in_specs=[pl.BlockSpec(memory_space=pltpu.SMEM)] * len(scalars) + (specs or whole),
        out_specs=out_specs or [pl.BlockSpec(memory_space=pltpu.VMEM)] * len(outs),
        out_shape=[(out[2] if len(out) > 2 else jax.ShapeDtypeStruct)(*out[:2]) for out in outs],
        compiler_params=pltpu.CompilerParams(vmem_limit_bytes=limit * MIB),
        cost_estimate=cost,
        **more,
    )(*scalars, *arrays)


def widen_kernel(router, wide):
    count, pieces, lanes = wide.shape
    row = router[...].astype(jnp.float32)
    row = [row[:, lanes * index : lanes * index + lanes] for index in range(pieces)]
    row = jnp.concatenate(row, axis=0)[None]
    wide[...] = jnp.broadcast_to(row, wide.shape).astype(wide.dtype)


def gather_router(router):
    wide = ((lax.axis_size(ALL), router.shape[1] // 128, 128), router.dtype, pltpu.HBM)
    wide = call(widen_kernel, [wide], [router])[0]
    return lax.all_to_all(wide, ALL, split_axis=0, concat_axis=0, tiled=True)


def hold_kernel(source, held, sem):
    copy = pltpu.make_async_copy(source, held, sem)
    copy.start()
    copy.wait()


def hold(array):
    return call(
        hold_kernel,
        [(array.shape, array.dtype, pltpu.VMEM)],
        [pltpu.with_memory_space_constraint(array, pltpu.HBM)],
        specs=[pl.BlockSpec(memory_space=pltpu.HBM)],
        scratch_shapes=[pltpu.SemaphoreType.DMA(())],
        cost=pl.CostEstimate(flops=10**6, bytes_accessed=8 * MIB, transcendentals=0),
    )[0]


def front_kernel(
    score_scale, high, tokens, received, d_out,
    wire, dispatch, combine, router_full, held_0, held_1, router, sems,
):
    for index in range(received.shape[1]):
        router[:, 128 * index : 128 * index + 128] = received[:, index]
    slots, grads = [], []
    for image in range(2):
        logits = product(tokens[image], router[...], 1, 1) * score_scale
        raised = jnp.exp(logits - jnp.max(logits, axis=0, keepdims=True))
        share = raised / jnp.sum(raised, axis=0, keepdims=True)
        held_0[image] = share
        slots.append(product(share.astype(wire.dtype), tokens[image], 0, 0).astype(wire.dtype))
        raised = jnp.exp(logits - jnp.max(logits, axis=1, keepdims=True))
        share = raised / jnp.sum(raised, axis=1, keepdims=True)
        held_1[image] = share
        grads.append(product(share.astype(wire.dtype), d_out[image], 0, 0).astype(wire.dtype))
    copies = [
        pltpu.make_async_copy(held_0, dispatch, sems.at[0]),
        pltpu.make_async_copy(held_1, combine, sems.at[1]),
        pltpu.make_async_copy(router, router_full, sems.at[2]),
    ]
    for copy in copies:
        copy.start()
    order = functools.partial(wire_from_slots, high[0])
    rows = [moved(order, jnp.concatenate(part, axis=0)) for part in (slots, grads)]
    rows = jnp.concatenate([part.reshape(32, 8, -1) for part in rows], axis=1)
    wire[...] = rows.astype(wire.dtype)
    for copy in copies:
        copy.wait()


def sort_kernel(wire, *parts):
    for core in range(2):
        rows = wire[16 * core : 16 * core + 16].reshape(256, -1)
        rows = moved(sorted_from_wire, rows).astype(wire.dtype)
        for index in range(8):
            part = parts[index // 2]
            part[index % 2, 32 * core : 32 * core + 32] = rows[32 * index : 32 * index + 32]


def stage_kernel(core, near_in, near_out, far_in, far_out, held_in, held_out, sems):
    copies = []
    for index, (weight, held) in enumerate(
        [(near_in, held_in), (near_out, held_out), (far_in, held_in), (far_out, held_out)]
    ):
        source = weight.at[pl.ds(2 * core[0], 2)]
        copies.append(pltpu.make_async_copy(source, held.at[index // 2], sems.at[index]))
    for copy in copies:
        copy.start()
    for copy in copies:
        copy.wait()


def stage(core, near_in, near_out, far_in, far_out):
    shards = [
        pltpu.with_memory_space_constraint(shard, pltpu.HBM)
        for shard in (near_in, near_out, far_in, far_out)
    ]
    shape = lambda shard: ((2, 2) + shard.shape[1:], shard.dtype, pltpu.VMEM)
    return call(
        stage_kernel,
        [shape(near_in), shape(near_out)],
        shards,
        [core],
        specs=[pl.BlockSpec(memory_space=pltpu.HBM)] * 4,
        scratch_shapes=[pltpu.SemaphoreType.DMA((4,))],
    )


def expert_kernel(chunk, *refs):
    blocks, (held_in, held_out), refs = refs[:4], refs[4:6], refs[6:]
    parts, (active, grads) = refs[:4], refs[4:]
    rows = jnp.concatenate([block[0] for block in blocks], axis=0)
    grad = jnp.concatenate([block[1] for block in blocks], axis=0)
    grads[...] = grad
    out = back = None
    for quarter in range(2):
        first, second = held_in[quarter, chunk], held_out[quarter, chunk]
        before = product(rows, first)
        below = 0.5 + 0.5 * lax.erf(before * math.sqrt(0.5))
        bell = jnp.exp(-0.5 * before * before) * (1.0 / math.sqrt(2.0 * math.pi))
        slope = below + before * bell
        rounded = (before * below).astype(active.dtype)
        active[quarter] = rounded
        part = product(rounded, second)
        out = part if out is None else out + part
        rounded = (product(grad, second, 1, 1) * slope).astype(grad.dtype)
        part = product(rounded, first, 1, 1)
        back = part if back is None else back + part
    for index, part in enumerate(parts):
        mine = slice(64 * index, 64 * index + 64)
        part[0] = out[mine].astype(part.dtype)
        part[1] = back[mine].astype(part.dtype)


def expert_call(chunk, blocks, held):
    half = jnp.bfloat16
    width, hidden = held[0].shape[2:]
    outs = [((2, 64, width), half, pltpu.VMEM)] * 4
    outs += [((2, 256, hidden), half), ((256, width), half)]
    held = [pltpu.with_memory_space_constraint(weight, pltpu.VMEM) for weight in held]
    return call(
        functools.partial(expert_kernel, chunk),
        outs,
        list(blocks) + held,
        cost=pl.CostEstimate(flops=8 * 10**9, bytes_accessed=24 * MIB, transcendentals=0),
    )


def sum_kernel(left, right, total):
    total[...] = (left[...].astype(jnp.float32) + right[...].astype(jnp.float32)).astype(total.dtype)


def sum_of(left, right):
    return call(sum_kernel, [(left.shape, left.dtype)], [left, right])[0]


def unsort_kernel(*refs):
    wire = refs[6]
    totals = []
    for index in range(2):
        own, pair, other = refs[3 * index : 3 * index + 3]
        total = own[...].astype(jnp.float32) + pair[...].astype(jnp.float32)
        totals += [total.astype(wire.dtype), other[...]]
    for core in range(2):
        mine = slice(32 * core, 32 * core + 32)
        rows = [total[tensor, mine] for total in totals for tensor in range(2)]
        rows = moved(wire_from_sorted, jnp.concatenate(rows, axis=0)).astype(wire.dtype)
        wire[16 * core : 16 * core + 16] = rows.reshape(16, 16, -1)


def score_kernel(
    score_scale, high, wire, tokens, d_out, dispatch, combine,
    logit_grad, slot_back, term, held_back, held_term, sems,
):
    rows = moved(functools.partial(slots_from_wire, high[0]), wire[...].reshape(512, -1))
    rows = rows.astype(wire.dtype)
    expert_out, back = rows[:256], rows[256:]
    held_back[...] = back
    copies = [
        pltpu.make_async_copy(held_back, slot_back, sems.at[0]),
        pltpu.make_async_copy(held_term, term, sems.at[1]),
    ]
    copies[0].start()
    total = None
    for image in range(2):
        mine = slice(128 * image, 128 * image + 128)
        grad = product(d_out[image], expert_out[mine], 1, 1)
        share = combine[image]
        score = share * (grad - jnp.sum(share * grad, axis=1, keepdims=True))
        grad = product(tokens[image], back[mine], 1, 1)
        share = dispatch[image]
        score = score + share * (grad - jnp.sum(share * grad, axis=0, keepdims=True))
        score = (score * score_scale).astype(logit_grad.dtype)
        logit_grad[image] = score
        part = product(score, tokens[image], 0, 0)
        total = part if total is None else total + part
    for index in range(term.shape[1]):
        held_term[:, index] = total[:, 128 * index : 128 * index + 128].astype(term.dtype)
    copies[1].start()
    for copy in copies:
        copy.wait()


def token_kernel(dispatch, logit_grad, slot_back, router, d_tokens):
    for image in range(2):
        mine = slice(128 * image, 128 * image + 128)
        total = product(dispatch[image].astype(slot_back.dtype), slot_back[mine])
        d_tokens[image] = (total + product(logit_grad[image], router[...])).astype(d_tokens.dtype)


def weight_kernel(chunk, core, active, grads, *refs):
    whole, away, held, sems = refs[-4:]
    copies = []
    for index, ref in enumerate((whole.at[2 * core[0] + chunk], away)):
        held[index] = product(active[index], grads[...], 0, 0).astype(held.dtype)
        copies.append(pltpu.make_async_copy(held.at[index], ref, sems.at[index]))
        copies[index].start()
    for copy in copies:
        copy.wait()


def weight_call(chunk, core, active, grads, *whole):
    shape = (active.shape[2], grads.shape[1])
    hbm = pl.BlockSpec(memory_space=pltpu.HBM)
    return call(
        functools.partial(weight_kernel, chunk),
        [((4,) + shape, grads.dtype, pltpu.HBM), (shape, grads.dtype, pltpu.HBM)],
        [active, grads, *whole],
        [core],
        specs=[pl.BlockSpec(memory_space=pltpu.VMEM)] * 2 + [hbm] * len(whole),
        out_specs=[hbm] * 2,
        scratch_shapes=[pltpu.VMEM((2,) + shape, grads.dtype), pltpu.SemaphoreType.DMA((2,))],
        input_output_aliases={3: 0} if whole else {},
    )


def gather_kernel(core, came_0, came_1, _, whole, held, sems):
    first = 2 - 2 * core[0]
    arrive = [
        pltpu.make_async_copy(came, held.at[index], sems.at[index])
        for index, came in enumerate((came_0, came_1))
    ]
    leave = [
        pltpu.make_async_copy(held.at[index], whole.at[first + index], sems.at[2 + index])
        for index in range(2)
    ]
    for copy in arrive:
        copy.start()
    for coming, going in zip(arrive, leave):
        coming.wait()
        going.start()
    for copy in leave:
        copy.wait()


def gather_call(core, came_0, came_1, whole):
    hbm = pl.BlockSpec(memory_space=pltpu.HBM)
    came = [pltpu.with_memory_space_constraint(part, pltpu.HBM) for part in (came_0, came_1)]
    return call(
        gather_kernel,
        [(whole.shape, whole.dtype, pltpu.HBM)],
        [*came, whole],
        [core],
        specs=[hbm] * 3,
        out_specs=[hbm],
        scratch_shapes=[
            pltpu.VMEM((2,) + whole.shape[1:], whole.dtype),
            pltpu.SemaphoreType.DMA((4,)),
        ],
        input_output_aliases={3: 0},
    )[0]


def body(tokens, router, w_in, w_out, d_out):
    images, count, width = tokens.shape
    slots = 128
    _, _, hidden = w_in.shape
    score_scale = 1.0 / math.sqrt(width)
    half = jnp.bfloat16
    high = lax.axis_index("zh").reshape(1).astype(jnp.int32)
    core = lax.axis_index("core").reshape(1).astype(jnp.int32)
    far_in = lax.ppermute(w_in, "core", SWAP)
    far_out = lax.ppermute(w_out, "core", SWAP)
    received = gather_router(router)
    held_tokens, held_out = hold(tokens), hold(d_out)
    (received,) = after(held_out, *after(held_tokens, received))
    rows = ((slots, width), half)
    weights = ((images, count, slots), jnp.float32)
    vmem = pl.BlockSpec(memory_space=pltpu.VMEM)
    hbm = pl.BlockSpec(memory_space=pltpu.HBM)
    wire, dispatch, combine, router_full = call(
        functools.partial(front_kernel, score_scale),
        [((32, 16, width), half)] + [kind + (pltpu.HBM,) for kind in (weights, weights, rows)],
        [pltpu.with_memory_space_constraint(part, pltpu.VMEM) for part in (held_tokens,)]
        + [received, pltpu.with_memory_space_constraint(held_out, pltpu.VMEM)],
        [high],
        out_specs=[vmem, hbm, hbm, hbm],
        scratch_shapes=[pltpu.VMEM(*kind) for kind in (weights, weights, rows)]
        + [pltpu.SemaphoreType.DMA((3,))],
    )
    (wire,) = after(far_out, *after(far_in, exchange(wire)))
    own_0, other_0, own_1, other_1 = call(
        sort_kernel,
        [((2, 64, width), half, kind) for kind in (pltpu.HBM, jax.ShapeDtypeStruct) * 2],
        [wire],
        cost=pl.CostEstimate(flops=10**6, bytes_accessed=40 * MIB, transcendentals=0),
    )
    pair_0, pair_1 = (lax.ppermute(own, "zl", SWAP) for own in (own_0, own_1))
    cross_0 = lax.ppermute(other_0, ("zl", "zh"), CROSS)
    cross_1 = lax.ppermute(other_1, ("zl", "zh"), CROSS)
    held = stage(core, *after(own_0, w_in, w_out, far_in, far_out))
    (cross_0,) = after(held[0], *after(pair_0, cross_0))
    (cross_1,) = after(pair_1, cross_1)
    far_0, far_1 = (lax.ppermute(cross, "zl", SWAP) for cross in (cross_0, cross_1))
    (far_0,) = after(cross_1, far_0)
    rows_0 = [own_0, pair_0, cross_0, far_0]
    rows_1 = [own_1, pair_1, cross_1, far_1]
    *parts_0, active_0, grads_0 = expert_call(0, rows_0, held)
    rows_1[3:] = after(parts_0[0], *rows_1[3:])
    *parts_1, active_1, grads_1 = expert_call(1, rows_1, held)
    far_0 = lax.ppermute(parts_0[3], "zl", SWAP)
    pair_0 = lax.ppermute(parts_0[1], "zl", SWAP)
    far_1 = lax.ppermute(parts_1[3], "zl", SWAP)
    pair_1 = lax.ppermute(parts_1[1], "zl", SWAP)
    (far_0,) = after(parts_1[0], far_0)
    cross_0 = sum_of(parts_0[2], far_0)
    other_0 = lax.ppermute(cross_0, ("zl", "zh"), CROSS)
    (active_0,) = after(cross_0, active_0)
    whole, away_0 = weight_call(0, core, active_0, grads_0)
    (far_1,) = after(away_0, far_1)
    cross_1 = sum_of(parts_1[2], far_1)
    other_1 = lax.ppermute(cross_1, ("zl", "zh"), CROSS)
    (active_1,) = after(pair_0, *after(cross_1, active_1))
    whole, away_1 = weight_call(1, core, active_1, grads_1, whole)
    other_0, other_1 = after(away_1, other_0, other_1)
    (away_0,) = after(away_1, away_0)
    came_0 = lax.ppermute(away_0, "core", SWAP)
    came_1 = lax.ppermute(away_1, "core", SWAP)
    wire = call(
        unsort_kernel,
        [((32, 16, width), half)],
        [parts_0[0], pair_0, other_0, parts_1[0], pair_1, other_1],
    )[0]
    wire = exchange(wire)

    logit_grad, slot_back, term = call(
        functools.partial(score_kernel, score_scale),
        [
            ((images, count, slots), half),
            ((images * slots, width), half, pltpu.HBM),
            ((slots, width // 128, 128), half, pltpu.HBM),
        ],
        [wire, tokens, d_out, dispatch, combine],
        [high],
        out_specs=[vmem, hbm, hbm],
        scratch_shapes=[
            pltpu.VMEM((images * slots, width), half),
            pltpu.VMEM((slots, width // 128, 128), half),
            pltpu.SemaphoreType.DMA((2,)),
        ],
    )
    received = lax.all_to_all(term, ALL, split_axis=0, concat_axis=0, tiled=True)
    d_router = jnp.sum(received.astype(jnp.float32), axis=0).reshape(1, -1)
    d_w_out = gather_call(core, *after(logit_grad, came_0, came_1), whole)
    (slot_back,) = after(d_w_out, slot_back)
    d_tokens = call(
        token_kernel,
        [((images, count, width), half)],
        [dispatch, logit_grad, slot_back, router_full],
    )[0]
    return (d_tokens, d_router, d_w_out)


def solution(mesh):
    split = jax.sharding.Mesh(mesh.devices.reshape(2, 2, 16, 2), ALL)
    dp, expert = ("zl", "core"), ("xy", "zh")
    placed = (
        P(ALL, None, None),
        P(ALL, None),
        P(expert, None, dp),
        P(expert, dp, None),
        P(ALL, None, None),
    )
    return jax.shard_map(
        body,
        mesh=split,
        in_specs=placed,
        out_specs=(P(ALL, None, None), P(ALL, None), P(expert, dp, None)),
        check_vma=False,
    )
```

```python
import functools
import math

import jax
import jax.numpy as jnp
from jax import lax
from jax.experimental import pallas as pl
from jax.experimental.pallas import tpu as pltpu
from jax.sharding import PartitionSpec as P

ALL = ("zl", "core", "xy", "zh")
PLANE = ("core", "xy")
SWAP = [(0, 1), (1, 0)]
CROSS = [(index, index ^ 3) for index in range(4)]
MIB = 2**20
FREE = pl.CostEstimate(flops=0, bytes_accessed=0, transcendentals=0)


def exchange(blocks):
    return lax.all_to_all(blocks, PLANE, split_axis=0, concat_axis=0, tiled=True)


def after(first, *later):
    return lax.optimization_barrier((first,) + later)[1:]


def product(left, right, left_dim=1, right_dim=0):
    dims = (((left_dim,), (right_dim,)), ((), ()))
    return lax.dot_general(left, right, dims, preferred_element_type=jnp.float32)


def moved(source_of, rows):
    count = rows.shape[0]
    source = source_of(lax.broadcasted_iota(jnp.int32, (count, count), 0))
    column = lax.broadcasted_iota(jnp.int32, (count, count), 1)
    pick = jnp.where(source == column, 1.0, 0.0).astype(rows.dtype)
    return product(pick, rows)


def bits(number, *widths):
    fields = []
    for width in reversed(widths):
        fields.append(number & ((1 << width) - 1))
        number = number >> width
    return fields[::-1]


def wire_from_slots(high, row):
    core, place, half, image, expert = bits(row, 1, 4, 1, 1, 1)
    return (image << 7) | (place << 3) | ((half ^ high) << 2) | (core << 1) | expert


def sorted_from_wire(row):
    expert, half, tensor, place, image = bits(row, 1, 1, 1, 4, 1)
    return (place << 4) | (tensor << 3) | (half << 2) | (image << 1) | expert


def wire_from_sorted(row):
    place, tensor, half, image, expert = bits(row, 4, 1, 1, 1, 1)
    return (expert << 7) | (half << 6) | (tensor << 5) | (place << 1) | image


def slots_from_wire(high, row):
    tensor, image, place, here, core, expert = bits(row, 1, 1, 4, 1, 1, 1)
    return (core << 8) | (place << 4) | (tensor << 3) | ((here ^ high) << 2) | (image << 1) | expert


def call(
    kernel, outs, arrays, scalars=(), limit=20, specs=None, out_specs=None, cost=FREE, **more
):
    whole = [pl.BlockSpec(memory_space=pltpu.VMEM)] * len(arrays)
    return pl.pallas_call(
        kernel,
        in_specs=[pl.BlockSpec(memory_space=pltpu.SMEM)] * len(scalars) + (specs or whole),
        out_specs=out_specs or [pl.BlockSpec(memory_space=pltpu.VMEM)] * len(outs),
        out_shape=[(out[2] if len(out) > 2 else jax.ShapeDtypeStruct)(*out[:2]) for out in outs],
        compiler_params=pltpu.CompilerParams(vmem_limit_bytes=limit * MIB),
        cost_estimate=cost,
        **more,
    )(*scalars, *arrays)


def widen_kernel(router, wide):
    count, pieces, lanes = wide.shape
    row = router[...].astype(jnp.float32)
    row = [row[:, lanes * index : lanes * index + lanes] for index in range(pieces)]
    row = jnp.concatenate(row, axis=0)[None]
    wide[...] = jnp.broadcast_to(row, wide.shape).astype(wide.dtype)


def gather_router(router):
    wide = ((lax.axis_size(ALL), 2, router.shape[1] // 2), router.dtype, pltpu.HBM)
    wide = call(widen_kernel, [wide], [router])[0]
    return lax.all_to_all(wide, ALL, split_axis=0, concat_axis=0, tiled=True)


def hold_kernel(source, held, sem):
    copy = pltpu.make_async_copy(source, held, sem)
    copy.start()
    copy.wait()


def hold(array):
    return call(
        hold_kernel,
        [(array.shape, array.dtype, pltpu.VMEM)],
        [pltpu.with_memory_space_constraint(array, pltpu.HBM)],
        specs=[pl.BlockSpec(memory_space=pltpu.HBM)],
        scratch_shapes=[pltpu.SemaphoreType.DMA(())],
        cost=pl.CostEstimate(flops=10**6, bytes_accessed=8 * MIB, transcendentals=0),
    )[0]


def front_kernel(
    score_scale, high, tokens, received, d_out,
    wire, dispatch, combine, router_full, held_0, held_1, router, sems,
):
    lanes = received.shape[2]
    for index in range(received.shape[1]):
        router[:, lanes * index : lanes * index + lanes] = received[:, index]
    slots, grads = [], []
    for image in range(2):
        logits = product(tokens[image], router[...], 1, 1) * score_scale
        raised = jnp.exp(logits - jnp.max(logits, axis=0, keepdims=True))
        share = raised / jnp.sum(raised, axis=0, keepdims=True)
        held_0[image] = share
        slots.append(product(share.astype(wire.dtype), tokens[image], 0, 0).astype(wire.dtype))
        raised = jnp.exp(logits - jnp.max(logits, axis=1, keepdims=True))
        share = raised / jnp.sum(raised, axis=1, keepdims=True)
        held_1[image] = share
        grads.append(product(share.astype(wire.dtype), d_out[image], 0, 0).astype(wire.dtype))
    copies = [
        pltpu.make_async_copy(held_0, dispatch, sems.at[0]),
        pltpu.make_async_copy(held_1, combine, sems.at[1]),
        pltpu.make_async_copy(router, router_full, sems.at[2]),
    ]
    for copy in copies:
        copy.start()
    order = functools.partial(wire_from_slots, high[0])
    rows = [moved(order, jnp.concatenate(part, axis=0)) for part in (slots, grads)]
    rows = jnp.concatenate([part.reshape(32, 8, -1) for part in rows], axis=1)
    wire[...] = rows.astype(wire.dtype)
    for copy in copies:
        copy.wait()


def sort_kernel(wire, *parts):
    for core in range(2):
        rows = wire[16 * core : 16 * core + 16].reshape(256, -1)
        rows = moved(sorted_from_wire, rows).astype(wire.dtype)
        for index in range(8):
            part = parts[index // 2]
            part[index % 2, 32 * core : 32 * core + 32] = rows[32 * index : 32 * index + 32]


def stage_kernel(core, near_in, near_out, far_in, far_out, held_in, held_out, sems):
    copies = []
    for index, (weight, held) in enumerate(
        [(near_in, held_in), (near_out, held_out), (far_in, held_in), (far_out, held_out)]
    ):
        source = weight.at[pl.ds(2 * core[0], 2)]
        copies.append(pltpu.make_async_copy(source, held.at[index // 2], sems.at[index]))
    for copy in copies:
        copy.start()
    for copy in copies:
        copy.wait()


def stage(core, near_in, near_out, far_in, far_out):
    shards = [
        pltpu.with_memory_space_constraint(shard, pltpu.HBM)
        for shard in (near_in, near_out, far_in, far_out)
    ]
    shape = lambda shard: ((2, 2) + shard.shape[1:], shard.dtype, pltpu.VMEM)
    return call(
        stage_kernel,
        [shape(near_in), shape(near_out)],
        shards,
        [core],
        specs=[pl.BlockSpec(memory_space=pltpu.HBM)] * 4,
        scratch_shapes=[pltpu.SemaphoreType.DMA((4,))],
    )


def expert_kernel(chunk, *refs):
    blocks, (held_in, held_out), refs = refs[:4], refs[4:6], refs[6:]
    parts, (active, grads) = refs[:4], refs[4:]
    rows = jnp.concatenate([block[0] for block in blocks], axis=0)
    grad = jnp.concatenate([block[1] for block in blocks], axis=0)
    grads[...] = grad
    out = back = None
    for quarter in range(2):
        first, second = held_in[quarter, chunk], held_out[quarter, chunk]
        before = product(rows, first)
        below = 0.5 + 0.5 * lax.erf(before * math.sqrt(0.5))
        bell = jnp.exp(-0.5 * before * before) * (1.0 / math.sqrt(2.0 * math.pi))
        slope = below + before * bell
        rounded = (before * below).astype(active.dtype)
        active[quarter] = rounded
        part = product(rounded, second)
        out = part if out is None else out + part
        rounded = (product(grad, second, 1, 1) * slope).astype(grad.dtype)
        part = product(rounded, first, 1, 1)
        back = part if back is None else back + part
    for index, part in enumerate(parts):
        mine = slice(64 * index, 64 * index + 64)
        part[0] = out[mine].astype(part.dtype)
        part[1] = back[mine].astype(part.dtype)


def expert_call(chunk, blocks, held):
    half = jnp.bfloat16
    width, hidden = held[0].shape[2:]
    outs = [((2, 64, width), half, pltpu.VMEM)] * 4
    outs += [((2, 256, hidden), half), ((256, width), half)]
    held = [pltpu.with_memory_space_constraint(weight, pltpu.VMEM) for weight in held]
    return call(
        functools.partial(expert_kernel, chunk),
        outs,
        list(blocks) + held,
        cost=pl.CostEstimate(flops=8 * 10**9, bytes_accessed=24 * MIB, transcendentals=0),
    )


def sum_kernel(left, right, total):
    total[...] = (left[...].astype(jnp.float32) + right[...].astype(jnp.float32)).astype(total.dtype)


def sum_of(left, right):
    return call(sum_kernel, [(left.shape, left.dtype)], [left, right])[0]


def unsort_kernel(*refs):
    wire = refs[6]
    totals = []
    for index in range(2):
        own, pair, other = refs[3 * index : 3 * index + 3]
        total = own[...].astype(jnp.float32) + pair[...].astype(jnp.float32)
        totals += [total.astype(wire.dtype), other[...]]
    for core in range(2):
        mine = slice(32 * core, 32 * core + 32)
        rows = [total[tensor, mine] for total in totals for tensor in range(2)]
        rows = moved(wire_from_sorted, jnp.concatenate(rows, axis=0)).astype(wire.dtype)
        wire[16 * core : 16 * core + 16] = rows.reshape(16, 16, -1)


def score_kernel(
    score_scale, high, wire, tokens, d_out, dispatch, combine,
    logit_grad, slot_back, term, held_back, held_term, sems,
):
    rows = moved(functools.partial(slots_from_wire, high[0]), wire[...].reshape(512, -1))
    rows = rows.astype(wire.dtype)
    expert_out, back = rows[:256], rows[256:]
    held_back[...] = back
    copies = [
        pltpu.make_async_copy(held_back, slot_back, sems.at[0]),
        pltpu.make_async_copy(held_term, term, sems.at[1]),
    ]
    copies[0].start()
    total = None
    for image in range(2):
        mine = slice(128 * image, 128 * image + 128)
        grad = product(d_out[image], expert_out[mine], 1, 1)
        share = combine[image]
        score = share * (grad - jnp.sum(share * grad, axis=1, keepdims=True))
        grad = product(tokens[image], back[mine], 1, 1)
        share = dispatch[image]
        score = score + share * (grad - jnp.sum(share * grad, axis=0, keepdims=True))
        score = (score * score_scale).astype(logit_grad.dtype)
        logit_grad[image] = score
        part = product(score, tokens[image], 0, 0)
        total = part if total is None else total + part
    lanes = term.shape[2]
    for index in range(term.shape[1]):
        held_term[:, index] = total[:, lanes * index : lanes * index + lanes].astype(term.dtype)
    copies[1].start()
    for copy in copies:
        copy.wait()


def token_kernel(dispatch, logit_grad, slot_back, router, d_tokens):
    for image in range(2):
        mine = slice(128 * image, 128 * image + 128)
        total = product(dispatch[image].astype(slot_back.dtype), slot_back[mine])
        d_tokens[image] = (total + product(logit_grad[image], router[...])).astype(d_tokens.dtype)


def weight_kernel(chunk, core, active, grads, *refs):
    whole, away, held, sems = refs[-4:]
    copies = []
    for index, ref in enumerate((whole.at[2 * core[0] + chunk], away)):
        held[index] = product(active[index], grads[...], 0, 0).astype(held.dtype)
        copies.append(pltpu.make_async_copy(held.at[index], ref, sems.at[index]))
        copies[index].start()
    for copy in copies:
        copy.wait()


def weight_call(chunk, core, active, grads, *whole):
    shape = (active.shape[2], grads.shape[1])
    hbm = pl.BlockSpec(memory_space=pltpu.HBM)
    return call(
        functools.partial(weight_kernel, chunk),
        [((4,) + shape, grads.dtype, pltpu.HBM), (shape, grads.dtype, pltpu.HBM)],
        [active, grads, *whole],
        [core],
        specs=[pl.BlockSpec(memory_space=pltpu.VMEM)] * 2 + [hbm] * len(whole),
        out_specs=[hbm] * 2,
        scratch_shapes=[pltpu.VMEM((2,) + shape, grads.dtype), pltpu.SemaphoreType.DMA((2,))],
        input_output_aliases={3: 0} if whole else {},
    )


def gather_kernel(core, came_0, came_1, _, whole, held, sems):
    first = 2 - 2 * core[0]
    arrive = [
        pltpu.make_async_copy(came, held.at[index], sems.at[index])
        for index, came in enumerate((came_0, came_1))
    ]
    leave = [
        pltpu.make_async_copy(held.at[index], whole.at[first + index], sems.at[2 + index])
        for index in range(2)
    ]
    for copy in arrive:
        copy.start()
    for coming, going in zip(arrive, leave):
        coming.wait()
        going.start()
    for copy in leave:
        copy.wait()


def gather_call(core, came_0, came_1, whole):
    hbm = pl.BlockSpec(memory_space=pltpu.HBM)
    came = [pltpu.with_memory_space_constraint(part, pltpu.HBM) for part in (came_0, came_1)]
    return call(
        gather_kernel,
        [(whole.shape, whole.dtype, pltpu.HBM)],
        [*came, whole],
        [core],
        specs=[hbm] * 3,
        out_specs=[hbm],
        scratch_shapes=[
            pltpu.VMEM((2,) + whole.shape[1:], whole.dtype),
            pltpu.SemaphoreType.DMA((4,)),
        ],
        input_output_aliases={3: 0},
    )[0]


def body(tokens, router, w_in, w_out, d_out):
    images, count, width = tokens.shape
    slots = 128
    _, _, hidden = w_in.shape
    score_scale = 1.0 / math.sqrt(width)
    half = jnp.bfloat16
    high = lax.axis_index("zh").reshape(1).astype(jnp.int32)
    core = lax.axis_index("core").reshape(1).astype(jnp.int32)
    far_in = lax.ppermute(w_in, "core", SWAP)
    far_out = lax.ppermute(w_out, "core", SWAP)
    received = gather_router(router)
    held_tokens, held_out = hold(tokens), hold(d_out)
    (received,) = after(held_out, *after(held_tokens, received))
    rows = ((slots, width), half)
    weights = ((images, count, slots), jnp.float32)
    vmem = pl.BlockSpec(memory_space=pltpu.VMEM)
    hbm = pl.BlockSpec(memory_space=pltpu.HBM)
    wire, dispatch, combine, router_full = call(
        functools.partial(front_kernel, score_scale),
        [((32, 16, width), half)] + [kind + (pltpu.HBM,) for kind in (weights, weights, rows)],
        [pltpu.with_memory_space_constraint(part, pltpu.VMEM) for part in (held_tokens,)]
        + [received, pltpu.with_memory_space_constraint(held_out, pltpu.VMEM)],
        [high],
        out_specs=[vmem, hbm, hbm, hbm],
        scratch_shapes=[pltpu.VMEM(*kind) for kind in (weights, weights, rows)]
        + [pltpu.SemaphoreType.DMA((3,))],
    )
    (wire,) = after(far_out, *after(far_in, exchange(wire)))
    own_0, other_0, own_1, other_1 = call(
        sort_kernel,
        [((2, 64, width), half, kind) for kind in (pltpu.HBM, jax.ShapeDtypeStruct) * 2],
        [wire],
        cost=pl.CostEstimate(flops=10**6, bytes_accessed=40 * MIB, transcendentals=0),
    )
    pair_0, pair_1 = (lax.ppermute(own, "zl", SWAP) for own in (own_0, own_1))
    cross_0 = lax.ppermute(other_0, ("zl", "zh"), CROSS)
    cross_1 = lax.ppermute(other_1, ("zl", "zh"), CROSS)
    held = stage(core, *after(own_0, w_in, w_out, far_in, far_out))
    (cross_0,) = after(held[0], *after(pair_0, cross_0))
    (cross_1,) = after(pair_1, cross_1)
    far_0, far_1 = (lax.ppermute(cross, "zl", SWAP) for cross in (cross_0, cross_1))
    (far_0,) = after(cross_1, far_0)
    rows_0 = [own_0, pair_0, cross_0, far_0]
    rows_1 = [own_1, pair_1, cross_1, far_1]
    *parts_0, active_0, grads_0 = expert_call(0, rows_0, held)
    rows_1[3:] = after(parts_0[0], *rows_1[3:])
    *parts_1, active_1, grads_1 = expert_call(1, rows_1, held)
    far_0 = lax.ppermute(parts_0[3], "zl", SWAP)
    pair_0 = lax.ppermute(parts_0[1], "zl", SWAP)
    far_1 = lax.ppermute(parts_1[3], "zl", SWAP)
    pair_1 = lax.ppermute(parts_1[1], "zl", SWAP)
    (far_0,) = after(parts_1[0], far_0)
    cross_0 = sum_of(parts_0[2], far_0)
    other_0 = lax.ppermute(cross_0, ("zl", "zh"), CROSS)
    (active_0,) = after(cross_0, active_0)
    whole, away_0 = weight_call(0, core, active_0, grads_0)
    (far_1,) = after(away_0, far_1)
    cross_1 = sum_of(parts_1[2], far_1)
    other_1 = lax.ppermute(cross_1, ("zl", "zh"), CROSS)
    (active_1,) = after(pair_0, *after(cross_1, active_1))
    whole, away_1 = weight_call(1, core, active_1, grads_1, whole)
    other_0, other_1 = after(away_1, other_0, other_1)
    (away_0,) = after(away_1, away_0)
    came_0 = lax.ppermute(away_0, "core", SWAP)
    came_1 = lax.ppermute(away_1, "core", SWAP)
    wire = call(
        unsort_kernel,
        [((32, 16, width), half)],
        [parts_0[0], pair_0, other_0, parts_1[0], pair_1, other_1],
    )[0]
    wire = exchange(wire)

    logit_grad, slot_back, term = call(
        functools.partial(score_kernel, score_scale),
        [
            ((images, count, slots), half),
            ((images * slots, width), half, pltpu.HBM),
            ((slots, 2, width // 2), half, pltpu.HBM),
        ],
        [wire, tokens, d_out, dispatch, combine],
        [high],
        out_specs=[vmem, hbm, hbm],
        scratch_shapes=[
            pltpu.VMEM((images * slots, width), half),
            pltpu.VMEM((slots, 2, width // 2), half),
            pltpu.SemaphoreType.DMA((2,)),
        ],
    )
    received = lax.all_to_all(term, ALL, split_axis=0, concat_axis=0, tiled=True)
    d_router = jnp.sum(received.astype(jnp.float32), axis=0).reshape(1, -1)
    d_w_out = gather_call(core, *after(logit_grad, came_0, came_1), whole)
    (slot_back,) = after(d_w_out, slot_back)
    d_tokens = call(
        token_kernel,
        [((images, count, width), half)],
        [dispatch, logit_grad, slot_back, router_full],
    )[0]
    return (d_tokens, d_router, d_w_out)


def solution(mesh):
    split = jax.sharding.Mesh(mesh.devices.reshape(2, 2, 16, 2), ALL)
    dp, expert = ("zl", "core"), ("xy", "zh")
    placed = (
        P(ALL, None, None),
        P(ALL, None),
        P(expert, None, dp),
        P(expert, dp, None),
        P(ALL, None, None),
    )
    return jax.shard_map(
        body,
        mesh=split,
        in_specs=placed,
        out_specs=(P(ALL, None, None), P(ALL, None), P(expert, dp, None)),
        check_vma=False,
    )
```
